512 devices in a mesh: ex: 16 (over y_lo, x, core), lay: 32 (over y_hi, z).
Axes of the slice: x: 4, y: 8 (y_hi: 4, y_lo: 2; y = y_hi * 2 + y_lo), z: 8, core: 2. Of those that a mesh axis runs over, the one named last changes fastest.
Arguments:
- query_grads: bfloat16 [512, 32, 4096], P('ex', 'lay'), may hold values from -6 to 6
- store: bfloat16 [8192, 32, 4096], P('ex', 'lay'), may hold values from -6 to 6
- left_inv: float32 [32, 64, 64], P('lay'), may hold values from -0.75 to 0.75
- right_inv: float32 [32, 64, 64], P('lay'), may hold values from -0.75 to 0.75
- query_ids: int32 [512], replicated, may hold values from 0 to 16383
- block_offsets: int32 [16], P('ex'), may hold values from 0 to 15872, as said below
Outputs:
- scores: float32 [512, 8192], P('lay', 'ex')
The draws below stay inside these ranges and needn't reach their ends.
Inputs may be any that keep to these rules, and one draw needn't show every extreme that they name: block_offsets[k] lies between 2 k * 512 and (2 k + 1) * 512, so the shards' ids never intersect.
All inputs are finite; a program needn't handle non-finite values.
Results may differ from the reference program's by a relative error of at most 0.0029.
Values may be sent and summed in bfloat16 or wider, within the bound.
A program may use at most 64 MiB of HBM per device.

```python
import jax
import jax.numpy as jnp
from jax import lax

R = 64
PROJ = 4096
LAYERS = 32
EX_DEV = 512
EXAMPLES = 8192
QUERIES = 512
N_EX = 16


def draw_block_offsets(key, part):
    key = jax.random.fold_in(key, 11)
    jitter = jax.random.randint(key, (N_EX,), 0, EX_DEV + 1)
    return (jnp.arange(N_EX, dtype=jnp.int32) * (2 * EX_DEV) + jitter).astype(jnp.int32)


def plant(values, key, smallest, high):
    longest = values.shape.index(max(values.shape))
    spots = []
    for shift in (0, 1):
        where = [jax.random.randint(jax.random.fold_in(key, axis), (), 0, length) for axis, length in enumerate(values.shape)]
        where[longest] = (where[longest] + shift) % values.shape[longest]
        spots.append(tuple(where))
    return values.at[spots[0]].set(smallest).at[spots[1]].set(high)


def steps_of(stream_key, shape, split, smallest, high):
    gain = 1.0
    for position, parts in split:
        steps = jax.random.uniform(jax.random.fold_in(jax.random.fold_in(stream_key, 6), position), (parts,), jnp.float32, smallest / len(split), high / len(split))
        gain = gain * jnp.repeat(jnp.exp(steps), shape[position] // parts).reshape((-1,) + (1,) * (len(shape) - 1 - position))
    return gain


def normal_values(key, shape, width, most, pieces=(), kind=jnp.bfloat16):
    factor_of = steps_of(key, shape, pieces, -0.22, 0.18) if pieces else 1.0
    entries = jax.random.normal(key, shape, jnp.float32) * width * factor_of
    return jnp.minimum(jnp.maximum(entries, -most), most).astype(kind)


def setup_inputs(seed: int = 0) -> dict:
    streams_of = jax.random.split(jax.random.key(seed), 7)
    query_grads = normal_values(streams_of[0], (QUERIES, LAYERS, PROJ), 1.0, 6.0, ((0, 16), (1, 32)))
    store = normal_values(streams_of[1], (EXAMPLES, LAYERS, PROJ), 1.0, 6.0, ((0, 16), (1, 32)))
    left_inv = normal_values(streams_of[2], (LAYERS, R, R), R ** -0.5, 0.75, ((0, 32),), jnp.float32)
    right_inv = normal_values(streams_of[3], (LAYERS, R, R), R ** -0.5, 0.75, ((0, 32),), jnp.float32)
    query_ids = plant(jax.random.randint(streams_of[4], (QUERIES,), 0, 2 * EXAMPLES), jax.random.fold_in(streams_of[4], 1), 0, (2 * EXAMPLES) - 1).astype(jnp.int32)
    block_offsets = draw_block_offsets(jax.random.fold_in(streams_of[6], 71), 0)
    return dict(query_grads=query_grads, store=store, left_inv=left_inv, right_inv=right_inv, query_ids=query_ids, block_offsets=block_offsets)


def condition(grads, left, right):
    count = grads.shape[0]
    mats = grads.astype(jnp.float32).reshape(count, R, R)
    out = jnp.einsum('ab,nbc,cd->nad', left, mats, right, precision=lax.Precision.HIGHEST)
    return out.reshape(count, R * R).astype(jnp.bfloat16)

def reference(query_grads, store, left_inv, right_inv, query_ids, block_offsets):

    def layer_step(carry, layer):
        partial_value, query_sq, example_sq = carry
        conditioned = condition(query_grads[:, layer, :], left_inv[layer], right_inv[layer])
        slab = store[:, layer, :]
        partial_value = partial_value + jnp.dot(conditioned, slab.T, preferred_element_type=jnp.float32)
        cond32 = conditioned.astype(jnp.float32)
        slab32 = slab.astype(jnp.float32)
        query_sq = query_sq + lax.optimization_barrier(jnp.sum(cond32 * cond32, axis=1))
        example_sq = example_sq + lax.optimization_barrier(jnp.sum(slab32 * slab32, axis=1))
        return ((partial_value, query_sq, example_sq), None)
    init = (jnp.zeros((QUERIES, EXAMPLES), jnp.float32), jnp.zeros((QUERIES,), jnp.float32), jnp.zeros((EXAMPLES,), jnp.float32))
    (partial_value, query_sq, example_sq), _ = lax.scan(layer_step, init, jnp.arange(LAYERS, dtype=jnp.int32))
    scale = jnp.sqrt(jnp.float32(LAYERS * PROJ))
    cosine = partial_value * lax.rsqrt(query_sq + 1e-06)[:, None] * lax.rsqrt(example_sq + 1e-06)[None, :] * scale
    positions = jnp.arange(EXAMPLES, dtype=jnp.int32)
    example_ids = jnp.repeat(block_offsets, EX_DEV) + positions % EX_DEV
    return jnp.where(query_ids[:, None] == example_ids[None, :], jnp.float32(0.0), cosine)
```

```python
import functools

import jax
import jax.numpy as jnp
from jax import lax
from jax.experimental import pallas as pl
from jax.experimental.pallas import tpu as pltpu
from jax.sharding import PartitionSpec as P

F32, BF16 = jnp.float32, jnp.bfloat16
MESH = pl.DeviceIdType.MESH
NT = (((1,), (1,)), ((), ()))
NN = (((1,), (0,)), ((), ()))

CHIPS = [(0, 0), (0, 1), (1, 0), (3, 0), (2, 0), (1, 1), (3, 1), (2, 1)]
BATCHES = [(0, 1), (1, 4), (4, 7), (7, 8)]
UNIT = 16
SIDE = 64


def slot(dx, dy):
    return CHIPS.index((dx % 4, dy % 2))


def unit(chip, other_core, half):
    return chip * 4 + other_core * 2 + half


def rows(u, n=1):
    return pl.ds(u * UNIT, n * UNIT)


def parts(value, n):
    out = []
    for _ in range(n):
        top = value.astype(BF16)
        out.append(top)
        value = value - top.astype(F32)
    return out


def dot(a, b, dims=NN):
    return lax.dot_general(a, b, dims, preferred_element_type=F32)


def condition(g_ref, left_ref, right_ref, mid_ref, out_ref, q_ref):
    count = g_ref.shape[0]
    pairs = SIDE // 2
    right = right_ref[...]
    wide = jnp.concatenate([right, right], axis=1)
    tall = jnp.concatenate([wide, wide], axis=0)
    row = lax.broadcasted_iota(jnp.int32, tall.shape, 0) < SIDE
    lane = lax.broadcasted_iota(jnp.int32, tall.shape, 1) < SIDE
    same = jnp.where(row == lane, tall, 0.0)
    cross = jnp.where(row == lane, 0.0, tall)
    both = jnp.concatenate([same, cross], axis=1)
    grads = jnp.concatenate([g_ref[:, p * 128 : (p + 1) * 128] for p in range(pairs)], axis=0)
    total = None
    for part in parts(both, 3):
        term = dot(grads, part)
        total = term if total is None else total + term
    mid_ref[0] = total[:, :128]
    mid_ref[1] = total[:, 128:]

    pick_r = lax.broadcasted_iota(jnp.int32, (SIDE, SIDE), 0)
    pick_c = lax.broadcasted_iota(jnp.int32, (SIDE, SIDE), 1)
    even_odd = jnp.where(pick_c < pairs, 2 * pick_c, 2 * (pick_c - pairs) + 1)
    odd_even = jnp.where(pick_c < pairs, 2 * pick_c + 1, 2 * (pick_c - pairs))
    to_eo = jnp.where(pick_r == even_odd, 1.0, 0.0).astype(BF16)
    to_oe = jnp.where(pick_r == odd_even, 1.0, 0.0).astype(BF16)
    out_ref[0:SIDE, 0:SIDE] = left_ref[...]
    even_rows = parts(out_ref[pl.ds(0, pairs, stride=2), :][:, :SIDE], 3)
    odd_rows = parts(out_ref[pl.ds(1, pairs, stride=2), :][:, :SIDE], 3)
    high, middle, low = [
        jnp.concatenate([dot(e, to_eo), dot(o, to_oe)], axis=0).astype(BF16)
        for e, o in zip(even_rows, odd_rows)
    ]
    left = jnp.concatenate([high, high, middle, middle, high, low], axis=1)

    lane2 = lax.broadcasted_iota(jnp.int32, (pairs, 256), 1) % 128 < SIDE
    for n in range(0, count, 2):
        columns = []
        for i in (n, n + 1):
            x = jnp.concatenate([mid_ref[t, pl.ds(i, pairs, stride=count), :] for t in range(2)], axis=0)
            xh, xm, xl = parts(x, 3)
            columns.append(jnp.concatenate([xh, xm, xh, xm, xl, xh], axis=0))
        res = dot(left, jnp.concatenate(columns, axis=1))
        res = jnp.where(lane2, res[:pairs], res[pairs:])
        out_ref[n * pairs : (n + 1) * pairs, :] = res[:, :128]
        out_ref[(n + 1) * pairs : (n + 2) * pairs, :] = res[:, 128:]

    squares = jnp.zeros((count, 128), F32)
    for p in range(pairs):
        value = out_ref[pl.ds(p, count, stride=pairs), :].astype(BF16)
        q_ref[0:count, p * 128 : (p + 1) * 128] = value
        wide_value = value.astype(F32)
        squares = squares + wide_value * wide_value
    return squares


def kernel(
    g_hbm, s_hbm, left_ref, right_ref, ids_ref, off_ref, out_ref,
    g_ref, s_ref, mid_ref, cond_ref, q_ref, p_ref, z_ref, ys_ref, yr_ref,
    nv_ref, nz_ref, ny_ref, nt_ref, nb_ref,
    load_sem, g_send, g_recv, z_send, z_recv, y_send, y_recv,
    nz_send, nz_recv, ny_send, ny_recv, nb_send, nb_recv,
):
    ex, lay = lax.axis_index("ex"), lax.axis_index("lay")
    core, x, yl = ex % 2, (ex // 2) % 4, ex // 8
    z, yh = lay % 8, lay // 8
    sibling = ex + 1 - 2 * core
    x_up = yl * 8 + ((x + 1) % 4) * 2 + core
    x_down = yl * 8 + ((x + 3) % 4) * 2 + core
    y_mate = (ex + 8) % 16

    barrier = pltpu.get_barrier_semaphore()
    for k in range(1, 16):
        pl.semaphore_signal(barrier, inc=1, device_id=((ex + k) % 16, lay), device_id_type=MESH)
    for k in range(1, 8):
        pl.semaphore_signal(barrier, inc=1, device_id=(ex, yh * 8 + (z + k) % 8), device_id_type=MESH)
    for k in range(1, 4):
        pl.semaphore_signal(barrier, inc=1, device_id=(ex, (lay + 8 * k) % 32), device_id_type=MESH)

    load_g = pltpu.make_async_copy(g_hbm, g_ref, load_sem.at[0])
    load_g.start()
    load_s = [
        pltpu.make_async_copy(s_hbm.at[pl.ds(128 * i, 128)], s_ref.at[pl.ds(128 * i, 128)], load_sem.at[1 + i])
        for i in range(4)
    ]
    for copy in load_s:
        copy.start()
    nv_ref[...] = jnp.zeros_like(nv_ref)
    load_g.wait()
    squares = condition(g_ref, left_ref, right_ref, mid_ref, cond_ref, q_ref)

    pl.semaphore_wait(barrier, 25)

    def send(src, dst, to):
        pltpu.make_async_remote_copy(
            src_ref=q_ref.at[rows(src)], dst_ref=q_ref.at[rows(dst)], send_sem=g_send.at[0],
            recv_sem=g_recv.at[dst], device_id=(to, lay), device_id_type=MESH,
        ).start()

    def arrived(u):
        pltpu.make_async_copy(q_ref.at[rows(u)], q_ref.at[rows(u)], g_recv.at[u]).wait()

    def up(dx, dy, half):
        send(unit(slot(dx, dy), 0, half), unit(slot(dx - 1, dy), 0, half), x_up)

    def down(dx, dy, half):
        send(unit(slot(dx, dy), 0, half), unit(slot(dx + 1, dy), 0, half), x_down)

    def across(dx, dy, half):
        send(unit(slot(dx, dy), 0, half), unit(slot(dx, dy + 1), 0, half), y_mate)

    def share(dx, dy, half):
        send(unit(slot(dx, dy), 0, half), unit(slot(dx, dy), 1, half), sibling)

    def take(dx, dy, half):
        arrived(unit(slot(dx, dy), 0, half))

    across(0, 0, 0)
    up(0, 0, 0)
    down(0, 0, 0)
    share(0, 0, 0)
    across(0, 0, 1)
    up(0, 0, 1)
    down(0, 0, 1)
    share(0, 0, 1)

    for copy in load_s:
        copy.wait()
    nv_ref[4:5, 0:32] = jnp.sum(squares.T, axis=0, keepdims=True)

    for block in range(4):
        pieces = []
        for part in range(2):
            total = jnp.zeros((64, 128), F32)
            for t in range(32):
                value = s_ref[block * 128 + part * 64 : block * 128 + part * 64 + 64, t * 128 : (t + 1) * 128].astype(F32)
                total = total + value * value
            pieces.append(total)
        nv_ref[block : block + 1, :] = jnp.sum(jnp.concatenate(pieces, axis=0).T, axis=0, keepdims=True)

    def z_norm(k):
        return pltpu.make_async_remote_copy(
            src_ref=nv_ref, dst_ref=nz_ref.at[k], send_sem=nz_send.at[k], recv_sem=nz_recv.at[k],
            device_id=(ex, yh * 8 + (z + k + 1) % 8), device_id_type=MESH,
        )

    for k in range(7):
        z_norm(k).start()

    def y_norm(k):
        return pltpu.make_async_remote_copy(
            src_ref=ny_ref.at[3], dst_ref=ny_ref.at[k], send_sem=ny_send.at[k], recv_sem=ny_recv.at[k],
            device_id=(ex, (lay + 8 * (k + 1)) % 32), device_id_type=MESH,
        )

    def b_norm(k):
        return pltpu.make_async_remote_copy(
            src_ref=nt_ref, dst_ref=nb_ref, send_sem=nb_send.at[k], recv_sem=nb_recv.at[0],
            device_id=((ex + k + 1) % 16, lay), device_id_type=MESH,
        )

    owner = lay // 2

    def norms_over_z():
        total = nv_ref[...]
        for k in range(7):
            z_norm(k).wait_recv()
            total = total + nz_ref[k]
        ny_ref[3] = total
        for k in range(3):
            y_norm(k).start()

    def norms_over_y():
        total = ny_ref[3]
        for k in range(3):
            y_norm(k).wait_recv()
            total = total + ny_ref[k]
        nt_ref[...] = total

        @pl.when(ex == owner)
        def _():
            for k in range(15):
                b_norm(k).start()

    def place(chip):
        dx, dy = CHIPS[chip]
        return (x + dx) % 4, (yl + dy) % 2

    def multiply(batch):
        first, last = BATCHES[batch]
        span = rows(first * 4, 4 * (last - first))
        p_ref[span, :] = dot(q_ref[span, :], s_ref[...], NT).astype(BF16)
        for chip in range(first, last):
            its_x, _ = place(chip)
            for other in range(2):
                for half in range(2):
                    u = unit(chip, other, half)
                    its_core = (core + other) % 2
                    goal = 4 * (its_x % 2) + 2 * its_core + half

                    @pl.when(goal != z)
                    def _():
                        pltpu.make_async_remote_copy(
                            src_ref=p_ref.at[rows(u)], dst_ref=z_ref.at[chip, (z + 8 - goal) % 8],
                            send_sem=z_send.at[chip], recv_sem=z_recv.at[chip],
                            device_id=(ex, yh * 8 + goal), device_id_type=MESH,
                        ).start()

    def mine(chip):
        its_x, _ = place(chip)
        return its_x % 2 == z // 4

    def goal_of(chip):
        its_x, its_y = place(chip)
        return 2 * its_y + its_x // 2

    def y_copy(chip):
        goal = goal_of(chip)
        return pltpu.make_async_remote_copy(
            src_ref=ys_ref.at[chip], dst_ref=yr_ref.at[(yh + 4 - goal) % 4],
            send_sem=y_send.at[chip], recv_sem=y_recv.at[(yh + 4 - goal) % 4],
            device_id=(ex, goal * 8 + z), device_id_type=MESH,
        )

    def sum_over_z(batch):
        first, last = BATCHES[batch]
        for chip in range(first, last):

            @pl.when(mine(chip))
            def _():
                pltpu.make_async_copy(
                    z_ref.at[chip, pl.ds(1, 7)], z_ref.at[chip, pl.ds(1, 7)], z_recv.at[chip]
                ).wait()
                within = (((z % 4) // 2 + core) % 2) * 2 + z % 2
                start = pl.multiple_of((chip * 4 + within) * UNIT, UNIT)
                total = p_ref[pl.ds(start, UNIT), :].astype(F32)
                for k in range(1, 8):
                    total = total + z_ref[chip, k].astype(F32)
                goal = goal_of(chip)

                @pl.when(goal == yh)
                def _():
                    yr_ref[0] = total

                @pl.when(goal != yh)
                def _():
                    ys_ref[chip] = total
                    y_copy(chip).start()

    arrived(unit(0, 1, 0))
    arrived(unit(0, 1, 1))
    multiply(0)

    take(0, 1, 0)
    up(0, 1, 0)
    down(0, 1, 0)
    share(0, 1, 0)
    take(3, 0, 0)
    up(3, 0, 0)
    share(3, 0, 0)
    take(1, 0, 0)
    share(1, 0, 0)
    norms_over_z()
    take(1, 0, 1)
    down(1, 0, 1)
    across(1, 0, 1)
    share(1, 0, 1)
    take(3, 0, 1)
    across(3, 0, 1)
    share(3, 0, 1)
    take(0, 1, 1)
    share(0, 1, 1)
    for chip in range(*BATCHES[1]):
        arrived(unit(chip, 1, 0))
        arrived(unit(chip, 1, 1))
    multiply(1)
    sum_over_z(0)

    take(2, 0, 0)
    share(2, 0, 0)
    take(2, 0, 1)
    across(2, 0, 1)
    share(2, 0, 1)
    take(3, 1, 0)

    @pl.when(core == 0)
    def _():
        up(3, 1, 0)

    share(3, 1, 0)
    take(1, 1, 0)

    @pl.when(core == 1)
    def _():
        down(1, 1, 0)

    share(1, 1, 0)
    norms_over_y()
    take(1, 1, 1)
    share(1, 1, 1)
    take(3, 1, 1)
    share(3, 1, 1)
    for chip in range(*BATCHES[2]):
        arrived(unit(chip, 1, 0))
        arrived(unit(chip, 1, 1))
    multiply(2)
    sum_over_z(1)

    take(2, 1, 0)
    share(2, 1, 0)
    take(2, 1, 1)
    share(2, 1, 1)
    arrived(unit(7, 1, 0))
    arrived(unit(7, 1, 1))
    multiply(3)
    sum_over_z(2)

    @pl.when(ex == owner)
    def _():
        nb_ref[...] = nt_ref[...]

    @pl.when(ex != owner)
    def _():
        b_norm(0).wait_recv()

    pltpu.make_async_copy(q_ref.at[rows(0, 30)], q_ref.at[rows(0, 30)], g_send.at[0]).wait()
    for k in range(7):
        z_norm(k).wait_send()
    for k in range(3):
        y_norm(k).wait_send()

    @pl.when(ex == owner)
    def _():
        for k in range(15):
            b_norm(k).wait_send()

    sum_over_z(3)
    for chip in range(8):

        @pl.when(mine(chip))
        def _():
            pltpu.make_async_copy(p_ref.at[rows(0, 3)], p_ref.at[rows(0, 3)], z_send.at[chip]).wait()

        @pl.when(jnp.logical_not(mine(chip)))
        def _():
            pltpu.make_async_copy(p_ref.at[rows(0, 4)], p_ref.at[rows(0, 4)], z_send.at[chip]).wait()

    columns = nb_ref[...].T[:, 4:5]
    query_sq = jnp.where(lay % 2 == 0, columns[:UNIT], columns[UNIT : 2 * UNIT])
    query_scale = lax.rsqrt(query_sq + 1e-06)
    scale = jnp.sqrt(F32(SIDE * SIDE * 32))
    which = lax.broadcasted_iota(jnp.int32, (UNIT, 128), 0)
    ids = jnp.zeros((UNIT, 128), jnp.int32)
    for i in range(UNIT):
        ids = jnp.where(which == i, ids_ref[lay * UNIT + i], ids)
    place_of = lax.broadcasted_iota(jnp.int32, (UNIT, 128), 1) + off_ref[0]
    for k in range(1, 4):
        pltpu.make_async_copy(yr_ref.at[k], yr_ref.at[k], y_recv.at[k]).wait()
    for block in range(4):
        span = slice(block * 128, (block + 1) * 128)
        total = yr_ref[0, :, span] + yr_ref[1, :, span] + yr_ref[2, :, span] + yr_ref[3, :, span]
        example_scale = lax.rsqrt(nt_ref[block : block + 1, :] + 1e-06)
        value = total * query_scale * example_scale * scale
        out_ref[:, span] = jnp.where(ids == place_of + block * 128, F32(0.0), value)
    for chip in range(8):

        @pl.when(jnp.logical_and(mine(chip), goal_of(chip) != yh))
        def _():
            y_copy(chip).wait_send()


def per_device(query_grads, store, left_inv, right_inv, query_ids, block_offsets):
    count, _, width = query_grads.shape
    examples = store.shape[0]
    vmem = pl.BlockSpec(memory_space=pltpu.VMEM)
    smem = pl.BlockSpec(memory_space=pltpu.SMEM)
    hbm = pl.BlockSpec(memory_space=pl.ANY)
    dma = pltpu.SemaphoreType.DMA
    return pl.pallas_call(
        kernel,
        out_shape=jax.ShapeDtypeStruct((UNIT, examples), F32),
        in_specs=[hbm, hbm, vmem, vmem, smem, smem],
        out_specs=vmem,
        scratch_shapes=[
            pltpu.VMEM((count, width), BF16),
            pltpu.VMEM((examples, width), BF16),
            pltpu.VMEM((2, 1024, 128), F32),
            pltpu.VMEM((1024, 128), F32),
            pltpu.VMEM((512, width), BF16),
            pltpu.VMEM((512, examples), BF16),
            pltpu.VMEM((8, 8, UNIT, examples), BF16),
            pltpu.VMEM((8, UNIT, examples), F32),
            pltpu.VMEM((4, UNIT, examples), F32),
            pltpu.VMEM((8, 128), F32),
            pltpu.VMEM((7, 8, 128), F32),
            pltpu.VMEM((4, 8, 128), F32),
            pltpu.VMEM((8, 128), F32),
            pltpu.VMEM((8, 128), F32),
            dma((5,)),
            dma((1,)),
            dma((32,)),
            dma((8,)),
            dma((8,)),
            dma((8,)),
            dma((4,)),
            dma((7,)),
            dma((7,)),
            dma((3,)),
            dma((3,)),
            dma((15,)),
            dma((1,)),
        ],
        compiler_params=pltpu.CompilerParams(
            collective_id=0, has_side_effects=True, vmem_limit_bytes=40 * 2**20
        ),
        cost_estimate=pl.CostEstimate(
            flops=2 * 512 * examples * width, bytes_accessed=(examples + count) * width * 2, transcendentals=0
        ),
    )(
        query_grads.reshape(count, width),
        store.reshape(examples, width),
        left_inv.reshape(SIDE, SIDE),
        right_inv.reshape(SIDE, SIDE),
        query_ids,
        block_offsets,
    )


def solution(mesh):
    return jax.shard_map(
        per_device,
        mesh=mesh,
        in_specs=(
            P("ex", "lay", None),
            P("ex", "lay", None),
            P("lay", None, None),
            P("lay", None, None),
            P(),
            P("ex"),
        ),
        out_specs=P("lay", "ex"),
        check_vma=False,
    )
```

```python
import functools

import jax
import jax.numpy as jnp
from jax import lax
from jax.experimental import pallas as pl
from jax.experimental.pallas import tpu as pltpu
from jax.sharding import PartitionSpec as P

F32, BF16 = jnp.float32, jnp.bfloat16
MESH = pl.DeviceIdType.MESH
NT = (((1,), (1,)), ((), ()))
NN = (((1,), (0,)), ((), ()))

CHIPS = [(0, 0), (0, 1), (1, 0), (3, 0), (2, 0), (1, 1), (3, 1), (2, 1)]
BATCHES = [
    [(0, 0, 0), (0, 0, 1)],
    [(1, 0, 1), (3, 0, 1), (0, 1, 1)],
    [(1, 0, 0), (3, 0, 0), (0, 1, 0)],
    [(2, 0, 1), (1, 1, 0), (3, 1, 0)],
    [(2, 0, 0), (1, 1, 1), (3, 1, 1)],
    [(2, 1, 0), (2, 1, 1)],
]
PLACES = [
    (dx, dy, other, half) for batch in BATCHES for other in range(2) for dx, dy, half in batch
]
UNIT = 16
SIDE = 64


def unit(dx, dy, other, half):
    return PLACES.index((dx % 4, dy % 2, other, half))


def rows(u, n=1):
    return pl.ds(u * UNIT, n * UNIT)


def parts(value, n):
    out = []
    for _ in range(n):
        top = value.astype(BF16)
        out.append(top)
        value = value - top.astype(F32)
    return out


def dot(a, b, dims=NN):
    return lax.dot_general(a, b, dims, preferred_element_type=F32)


def factors(left_ref, right_ref, tmp_ref):
    pairs = SIDE // 2
    right = right_ref[...]
    wide = jnp.concatenate([right, right], axis=1)
    tall = jnp.concatenate([wide, wide], axis=0)
    row = lax.broadcasted_iota(jnp.int32, tall.shape, 0) < SIDE
    lane = lax.broadcasted_iota(jnp.int32, tall.shape, 1) < SIDE
    same = jnp.where(row == lane, tall, 0.0)
    cross = jnp.where(row == lane, 0.0, tall)
    right_parts = parts(jnp.concatenate([same, cross], axis=1), 3)

    pick_r = lax.broadcasted_iota(jnp.int32, (SIDE, SIDE), 0)
    pick_c = lax.broadcasted_iota(jnp.int32, (SIDE, SIDE), 1)
    even_odd = jnp.where(pick_c < pairs, 2 * pick_c, 2 * (pick_c - pairs) + 1)
    odd_even = jnp.where(pick_c < pairs, 2 * pick_c + 1, 2 * (pick_c - pairs))
    to_eo = jnp.where(pick_r == even_odd, 1.0, 0.0).astype(BF16)
    to_oe = jnp.where(pick_r == odd_even, 1.0, 0.0).astype(BF16)
    tmp_ref[0:SIDE, :] = jnp.concatenate([left_ref[...], jnp.zeros((SIDE, SIDE), F32)], axis=1)
    even_rows = parts(tmp_ref[pl.ds(0, pairs, stride=2), :][:, :SIDE], 3)
    odd_rows = parts(tmp_ref[pl.ds(1, pairs, stride=2), :][:, :SIDE], 3)
    high, middle, low = [
        jnp.concatenate([dot(e, to_eo), dot(o, to_oe)], axis=0).astype(BF16)
        for e, o in zip(even_rows, odd_rows)
    ]
    left = jnp.concatenate([high, high, middle, middle, high, low], axis=1)
    return left, right_parts


def condition(g_ref, half, left, right_parts, mid_ref, tmp_ref, q_ref):
    pairs = SIDE // 2
    mine = slice(half * UNIT, (half + 1) * UNIT)
    grads = jnp.concatenate([g_ref[mine, p * 128 : (p + 1) * 128] for p in range(pairs)], axis=0)
    total = None
    for part in right_parts:
        term = dot(grads, part)
        total = term if total is None else total + term
    mid_ref[0] = total[:, :128]
    mid_ref[1] = total[:, 128:]
    lane = lax.broadcasted_iota(jnp.int32, (pairs, 256), 1) % 128 < SIDE
    for n in range(0, UNIT, 2):
        columns = []
        for i in (n, n + 1):
            x = jnp.concatenate([mid_ref[t, pl.ds(i, pairs, stride=UNIT), :] for t in range(2)], axis=0)
            xh, xm, xl = parts(x, 3)
            columns.append(jnp.concatenate([xh, xm, xh, xm, xl, xh], axis=0))
        res = dot(left, jnp.concatenate(columns, axis=1))
        res = jnp.where(lane, res[:pairs], res[pairs:])
        tmp_ref[n * pairs : (n + 1) * pairs, :] = res[:, :128]
        tmp_ref[(n + 1) * pairs : (n + 2) * pairs, :] = res[:, 128:]
    squares = jnp.zeros((UNIT, 128), F32)
    for p in range(pairs):
        value = tmp_ref[pl.ds(p, UNIT, stride=pairs), :].astype(BF16)
        q_ref[mine, p * 128 : (p + 1) * 128] = value
        wide_value = value.astype(F32)
        squares = squares + wide_value * wide_value
    return squares


def kernel(
    g_hbm, s_hbm, left_hbm, right_hbm, ids_hbm, off_ref, out_ref,
    g_ref, s_ref, left_ref, right_ref, ids_ref, mid_ref, cond_ref, q_ref, p_ref, z_ref, ys_ref, yr_ref,
    nv_ref, nz_ref, ny_ref, nt_ref, nb_ref,
    load_sem, g_send, g_recv, z_send, z_recv, y_send, y_recv,
    nz_send, nz_recv, ny_send, ny_recv, nb_send, nb_recv,
):
    ex, lay = lax.axis_index("ex"), lax.axis_index("lay")
    core, x, yl = ex % 2, (ex // 2) % 4, ex // 8
    z, yh = lay % 8, lay // 8
    sibling = ex + 1 - 2 * core
    x_up = yl * 8 + ((x + 1) % 4) * 2 + core
    x_down = yl * 8 + ((x + 3) % 4) * 2 + core
    y_mate = (ex + 8) % 16

    barrier = pltpu.get_barrier_semaphore()
    for k in range(1, 16):
        pl.semaphore_signal(barrier, inc=1, device_id=((ex + k) % 16, lay), device_id_type=MESH)
    for k in range(1, 8):
        pl.semaphore_signal(barrier, inc=1, device_id=(ex, yh * 8 + (z + k) % 8), device_id_type=MESH)
    for k in range(1, 4):
        pl.semaphore_signal(barrier, inc=1, device_id=(ex, (lay + 8 * k) % 32), device_id_type=MESH)

    first = [
        pltpu.make_async_copy(src, dst, load_sem.at[4 + i])
        for i, (src, dst) in enumerate([(right_hbm, right_ref), (g_hbm, g_ref), (left_hbm, left_ref)])
    ]
    small = [pltpu.make_async_copy(ids_hbm, ids_ref, load_sem.at[7])]
    for copy in first:
        copy.start()
    load_s = [
        pltpu.make_async_copy(s_hbm.at[pl.ds(128 * i, 128)], s_ref.at[pl.ds(128 * i, 128)], load_sem.at[i])
        for i in range(4)
    ]
    for copy in load_s + small:
        copy.start()
    nv_ref[...] = jnp.zeros_like(nv_ref)
    for copy in first:
        copy.wait()
    left, right_parts = factors(left_ref, right_ref, cond_ref.at[1])
    squares_1 = condition(g_ref, 1, left, right_parts, mid_ref.at[1], cond_ref.at[1], q_ref)

    pl.semaphore_wait(barrier, 25)

    def send(src, dst, to):
        pltpu.make_async_remote_copy(
            src_ref=q_ref.at[rows(src)], dst_ref=q_ref.at[rows(dst)], send_sem=g_send.at[0],
            recv_sem=g_recv.at[dst], device_id=(to, lay), device_id_type=MESH,
        ).start()

    def arrived(u):
        pltpu.make_async_copy(q_ref.at[rows(u)], q_ref.at[rows(u)], g_recv.at[u]).wait()

    def up(dx, dy, half):
        send(unit(dx, dy, 0, half), unit(dx - 1, dy, 0, half), x_up)

    def down(dx, dy, half):
        send(unit(dx, dy, 0, half), unit(dx + 1, dy, 0, half), x_down)

    def across(dx, dy, half):
        send(unit(dx, dy, 0, half), unit(dx, dy + 1, 0, half), y_mate)

    def share(dx, dy, half):
        send(unit(dx, dy, 0, half), unit(dx, dy, 1, half), sibling)

    def take(dx, dy, half):
        arrived(unit(dx, dy, 0, half))

    up(0, 0, 1)
    down(0, 0, 1)
    across(0, 0, 1)
    share(0, 0, 1)
    squares_0 = condition(g_ref, 0, left, right_parts, mid_ref.at[0], cond_ref.at[0], q_ref)
    across(0, 0, 0)
    up(0, 0, 0)
    down(0, 0, 0)
    share(0, 0, 0)
    squares = jnp.concatenate([squares_0, squares_1], axis=0)

    for copy in load_s + small:
        copy.wait()
    nv_ref[4:5, 0:32] = jnp.sum(squares.T, axis=0, keepdims=True)

    for block in range(4):
        pieces = []
        for part in range(2):
            total = jnp.zeros((64, 128), F32)
            for t in range(32):
                value = s_ref[block * 128 + part * 64 : block * 128 + part * 64 + 64, t * 128 : (t + 1) * 128].astype(F32)
                total = total + value * value
            pieces.append(total)
        nv_ref[block : block + 1, :] = jnp.sum(jnp.concatenate(pieces, axis=0).T, axis=0, keepdims=True)

    def z_norm(k):
        return pltpu.make_async_remote_copy(
            src_ref=nv_ref, dst_ref=nz_ref.at[k], send_sem=nz_send.at[k], recv_sem=nz_recv.at[k],
            device_id=(ex, yh * 8 + (z + k + 1) % 8), device_id_type=MESH,
        )

    for k in range(7):
        z_norm(k).start()

    def y_norm(k):
        return pltpu.make_async_remote_copy(
            src_ref=ny_ref.at[3], dst_ref=ny_ref.at[k], send_sem=ny_send.at[k], recv_sem=ny_recv.at[k],
            device_id=(ex, (lay + 8 * (k + 1)) % 32), device_id_type=MESH,
        )

    def b_norm(k):
        return pltpu.make_async_remote_copy(
            src_ref=nt_ref, dst_ref=nb_ref, send_sem=nb_send.at[k], recv_sem=nb_recv.at[0],
            device_id=((ex + k + 1) % 16, lay), device_id_type=MESH,
        )

    owner = lay // 2

    def norms_over_z():
        total = nv_ref[...]
        for k in range(7):
            z_norm(k).wait_recv()
            total = total + nz_ref[k]
        ny_ref[3] = total
        for k in range(3):
            y_norm(k).start()

    def norms_over_y():
        total = ny_ref[3]
        for k in range(3):
            y_norm(k).wait_recv()
            total = total + ny_ref[k]
        nt_ref[...] = total

        @pl.when(ex == owner)
        def _():
            for k in range(15):
                b_norm(k).start()

    def place(chip):
        dx, dy = CHIPS[chip]
        return (x + dx) % 4, (yl + dy) % 2

    def multiply(batch):
        first = PLACES.index(BATCHES[batch][0][:2] + (0,) + BATCHES[batch][0][2:])
        for dx, dy, half in BATCHES[batch]:
            arrived(unit(dx, dy, 1, half))
        span = rows(first, 2 * len(BATCHES[batch]))
        p_ref[span, :] = dot(q_ref[span, :], s_ref[...], NT).astype(BF16)
        for dx, dy, half in BATCHES[batch]:
            chip = CHIPS.index((dx, dy))
            for other in range(2):
                u = unit(dx, dy, other, half)
                goal = 4 * ((x + dx) % 2) + 2 * ((core + other) % 2) + half

                @pl.when(goal != z)
                def _():
                    pltpu.make_async_remote_copy(
                        src_ref=p_ref.at[rows(u)], dst_ref=z_ref.at[chip, (z + 8 - goal) % 8],
                        send_sem=z_send.at[chip], recv_sem=z_recv.at[chip],
                        device_id=(ex, yh * 8 + goal), device_id_type=MESH,
                    ).start()

                @pl.when(goal == z)
                def _():
                    z_ref[chip, 0] = p_ref[rows(u), :]

    def mine(chip):
        its_x, _ = place(chip)
        return its_x % 2 == z // 4

    def goal_of(chip):
        its_x, its_y = place(chip)
        return 2 * its_y + its_x // 2

    def y_copy(chip):
        goal = goal_of(chip)
        return pltpu.make_async_remote_copy(
            src_ref=ys_ref.at[chip], dst_ref=yr_ref.at[(yh + 4 - goal) % 4],
            send_sem=y_send.at[chip], recv_sem=y_recv.at[(yh + 4 - goal) % 4],
            device_id=(ex, goal * 8 + z), device_id_type=MESH,
        )

    def sum_over_z(dx, dy):
        chip = CHIPS.index((dx, dy))

        @pl.when(mine(chip))
        def _():
            pltpu.make_async_copy(
                z_ref.at[chip, pl.ds(1, 7)], z_ref.at[chip, pl.ds(1, 7)], z_recv.at[chip]
            ).wait()
            total = z_ref[chip, 0].astype(F32)
            for k in range(1, 8):
                total = total + z_ref[chip, k].astype(F32)
            goal = goal_of(chip)

            @pl.when(goal == yh)
            def _():
                yr_ref[0] = total

            @pl.when(goal != yh)
            def _():
                ys_ref[chip] = total
                y_copy(chip).start()

    multiply(0)

    take(3, 0, 1)
    take(1, 0, 1)

    @pl.when(core == 0)
    def _():
        up(3, 0, 1)
        across(1, 0, 1)
        across(3, 0, 1)

    @pl.when(core == 1)
    def _():
        down(1, 0, 1)
        across(3, 0, 1)
        across(1, 0, 1)

    share(3, 0, 1)
    share(1, 0, 1)
    take(0, 1, 1)
    share(0, 1, 1)
    multiply(1)

    take(0, 1, 0)
    up(0, 1, 0)
    down(0, 1, 0)
    share(0, 1, 0)
    take(3, 0, 0)
    take(1, 0, 0)

    @pl.when(core == 0)
    def _():
        down(1, 0, 0)

    @pl.when(core == 1)
    def _():
        up(3, 0, 0)

    share(3, 0, 0)
    share(1, 0, 0)
    norms_over_z()
    sum_over_z(0, 0)
    multiply(2)

    take(2, 0, 1)
    share(2, 0, 1)

    @pl.when(core == 0)
    def _():
        take(1, 1, 1)
        down(1, 1, 1)
        share(1, 1, 1)

    @pl.when(core == 1)
    def _():
        take(3, 1, 1)
        up(3, 1, 1)
        share(3, 1, 1)

    take(3, 1, 0)
    take(1, 1, 0)

    @pl.when(core == 0)
    def _():
        up(3, 1, 0)

    @pl.when(core == 1)
    def _():
        down(1, 1, 0)

    share(3, 1, 0)
    share(1, 1, 0)
    multiply(3)
    take(2, 0, 0)
    share(2, 0, 0)

    @pl.when(core == 0)
    def _():
        take(3, 1, 1)
        share(3, 1, 1)

    @pl.when(core == 1)
    def _():
        take(1, 1, 1)
        share(1, 1, 1)

    norms_over_y()
    sum_over_z(0, 1)
    sum_over_z(1, 0)
    sum_over_z(3, 0)
    multiply(4)

    take(2, 1, 0)
    share(2, 1, 0)
    take(2, 1, 1)
    share(2, 1, 1)
    multiply(5)
    sum_over_z(2, 0)
    sum_over_z(1, 1)
    sum_over_z(3, 1)

    @pl.when(ex == owner)
    def _():
        nb_ref[...] = nt_ref[...]

    @pl.when(ex != owner)
    def _():
        b_norm(0).wait_recv()

    pltpu.make_async_copy(q_ref.at[rows(0, 30)], q_ref.at[rows(0, 30)], g_send.at[0]).wait()
    for k in range(7):
        z_norm(k).wait_send()
    for k in range(3):
        y_norm(k).wait_send()

    @pl.when(ex == owner)
    def _():
        for k in range(15):
            b_norm(k).wait_send()

    sum_over_z(2, 1)
    for chip in range(8):

        @pl.when(mine(chip))
        def _():
            pltpu.make_async_copy(p_ref.at[rows(0, 3)], p_ref.at[rows(0, 3)], z_send.at[chip]).wait()

        @pl.when(jnp.logical_not(mine(chip)))
        def _():
            pltpu.make_async_copy(p_ref.at[rows(0, 4)], p_ref.at[rows(0, 4)], z_send.at[chip]).wait()

    columns = nb_ref[...].T[:, 4:5]
    query_sq = jnp.where(lay % 2 == 0, columns[:UNIT], columns[UNIT : 2 * UNIT])
    query_scale = lax.rsqrt(query_sq + 1e-06)
    scale = jnp.sqrt(F32(SIDE * SIDE * 32))
    which = lax.broadcasted_iota(jnp.int32, (UNIT, 128), 0)
    ids = jnp.zeros((UNIT, 128), jnp.int32)
    for i in range(UNIT):
        ids = jnp.where(which == i, ids_ref[lay * UNIT + i], ids)
    place_of = lax.broadcasted_iota(jnp.int32, (UNIT, 128), 1) + off_ref[0]
    for k in range(1, 4):
        pltpu.make_async_copy(yr_ref.at[k], yr_ref.at[k], y_recv.at[k]).wait()
    for block in range(4):
        span = slice(block * 128, (block + 1) * 128)
        total = yr_ref[0, :, span] + yr_ref[1, :, span] + yr_ref[2, :, span] + yr_ref[3, :, span]
        example_scale = lax.rsqrt(nt_ref[block : block + 1, :] + 1e-06)
        value = total * query_scale * example_scale * scale
        out_ref[:, span] = jnp.where(ids == place_of + block * 128, F32(0.0), value)
    for chip in range(8):

        @pl.when(jnp.logical_and(mine(chip), goal_of(chip) != yh))
        def _():
            y_copy(chip).wait_send()


def per_device(query_grads, store, left_inv, right_inv, query_ids, block_offsets):
    count, _, width = query_grads.shape
    examples = store.shape[0]
    vmem = pl.BlockSpec(memory_space=pltpu.VMEM)
    hbm = pl.BlockSpec(memory_space=pltpu.HBM)
    dma = pltpu.SemaphoreType.DMA
    return pl.pallas_call(
        kernel,
        out_shape=jax.ShapeDtypeStruct((UNIT, examples), F32),
        in_specs=[hbm] * 5 + [pl.BlockSpec(memory_space=pltpu.SMEM)],
        out_specs=vmem,
        scratch_shapes=[
            pltpu.VMEM((count, width), BF16),
            pltpu.VMEM((examples, width), BF16),
            pltpu.VMEM((SIDE, SIDE), F32),
            pltpu.VMEM((SIDE, SIDE), F32),
            pltpu.SMEM(query_ids.shape, jnp.int32),
            pltpu.VMEM((2, 2, 512, 128), F32),
            pltpu.VMEM((2, 512, 128), F32),
            pltpu.VMEM((512, width), BF16),
            pltpu.VMEM((512, examples), BF16),
            pltpu.VMEM((8, 8, UNIT, examples), BF16),
            pltpu.VMEM((8, UNIT, examples), F32),
            pltpu.VMEM((4, UNIT, examples), F32),
            pltpu.VMEM((8, 128), F32),
            pltpu.VMEM((7, 8, 128), F32),
            pltpu.VMEM((4, 8, 128), F32),
            pltpu.VMEM((8, 128), F32),
            pltpu.VMEM((8, 128), F32),
            dma((8,)),
            dma((1,)),
            dma((32,)),
            dma((8,)),
            dma((8,)),
            dma((8,)),
            dma((4,)),
            dma((7,)),
            dma((7,)),
            dma((3,)),
            dma((3,)),
            dma((15,)),
            dma((1,)),
        ],
        compiler_params=pltpu.CompilerParams(
            collective_id=0, has_side_effects=True, vmem_limit_bytes=60 * 2**20
        ),
        cost_estimate=pl.CostEstimate(
            flops=2 * 512 * examples * width, bytes_accessed=(examples + count) * width * 2, transcendentals=0
        ),
    )(
        query_grads.reshape(count, width),
        store.reshape(examples, width),
        left_inv.reshape(SIDE, SIDE),
        right_inv.reshape(SIDE, SIDE),
        query_ids,
        block_offsets,
    )


def solution(mesh):
    return jax.shard_map(
        per_device,
        mesh=mesh,
        in_specs=(
            P("ex", "lay", None),
            P("ex", "lay", None),
            P("lay", None, None),
            P("lay", None, None),
            P(),
            P("ex"),
        ),
        out_specs=P("lay", "ex"),
        check_vma=False,
    )
```

```python
import functools

import jax
import jax.numpy as jnp
from jax import lax
from jax.experimental import pallas as pl
from jax.experimental.pallas import tpu as pltpu
from jax.sharding import PartitionSpec as P

F32, BF16 = jnp.float32, jnp.bfloat16
MESH = pl.DeviceIdType.MESH
NT = (((1,), (1,)), ((), ()))
NN = (((1,), (0,)), ((), ()))

CHIPS = [(0, 0), (0, 1), (1, 0), (3, 0), (2, 0), (1, 1), (3, 1), (2, 1)]
BATCHES = [
    [(0, 0, 0), (0, 0, 1)],
    [(1, 0, 1), (3, 0, 1), (0, 1, 1), (1, 0, 0), (3, 0, 0), (0, 1, 0)],
    [(2, 0, 1), (1, 1, 0), (3, 1, 0), (2, 0, 0), (1, 1, 1), (3, 1, 1)],
    [(2, 1, 0), (2, 1, 1)],
]
PLACES = [
    (dx, dy, other, half) for batch in BATCHES for other in range(2) for dx, dy, half in batch
]
UNIT = 16
SIDE = 64


def unit(dx, dy, other, half):
    return PLACES.index((dx % 4, dy % 2, other, half))


def rows(u, n=1):
    return pl.ds(u * UNIT, n * UNIT)


def parts(value, n):
    out = []
    for _ in range(n):
        top = value.astype(BF16)
        out.append(top)
        value = value - top.astype(F32)
    return out


def dot(a, b, dims=NN):
    return lax.dot_general(a, b, dims, preferred_element_type=F32)


def factors(left_ref, right_ref, tmp_ref):
    pairs = SIDE // 2
    right = right_ref[...]
    wide = jnp.concatenate([right, right], axis=1)
    tall = jnp.concatenate([wide, wide], axis=0)
    row = lax.broadcasted_iota(jnp.int32, tall.shape, 0) < SIDE
    lane = lax.broadcasted_iota(jnp.int32, tall.shape, 1) < SIDE
    same = jnp.where(row == lane, tall, 0.0)
    cross = jnp.where(row == lane, 0.0, tall)
    right_parts = parts(jnp.concatenate([same, cross], axis=1), 3)

    pick_r = lax.broadcasted_iota(jnp.int32, (SIDE, SIDE), 0)
    pick_c = lax.broadcasted_iota(jnp.int32, (SIDE, SIDE), 1)
    even_odd = jnp.where(pick_c < pairs, 2 * pick_c, 2 * (pick_c - pairs) + 1)
    odd_even = jnp.where(pick_c < pairs, 2 * pick_c + 1, 2 * (pick_c - pairs))
    to_eo = jnp.where(pick_r == even_odd, 1.0, 0.0).astype(BF16)
    to_oe = jnp.where(pick_r == odd_even, 1.0, 0.0).astype(BF16)
    tmp_ref[0:SIDE, :] = jnp.concatenate([left_ref[...], jnp.zeros((SIDE, SIDE), F32)], axis=1)
    even_rows = parts(tmp_ref[pl.ds(0, pairs, stride=2), :][:, :SIDE], 3)
    odd_rows = parts(tmp_ref[pl.ds(1, pairs, stride=2), :][:, :SIDE], 3)
    high, middle, low = [
        jnp.concatenate([dot(e, to_eo), dot(o, to_oe)], axis=0).astype(BF16)
        for e, o in zip(even_rows, odd_rows)
    ]
    left = jnp.concatenate([high, high, middle, middle, high, low], axis=1)
    return left, right_parts


def condition(g_ref, half, left, right_parts, mid_ref, tmp_ref, q_ref):
    pairs = SIDE // 2
    mine = slice(half * UNIT, (half + 1) * UNIT)
    grads = jnp.concatenate([g_ref[mine, p * 128 : (p + 1) * 128] for p in range(pairs)], axis=0)
    total = None
    for part in right_parts:
        term = dot(grads, part)
        total = term if total is None else total + term
    mid_ref[0] = total[:, :128]
    mid_ref[1] = total[:, 128:]
    lane = lax.broadcasted_iota(jnp.int32, (pairs, 256), 1) % 128 < SIDE
    for n in range(0, UNIT, 2):
        columns = []
        for i in (n, n + 1):
            x = jnp.concatenate([mid_ref[t, pl.ds(i, pairs, stride=UNIT), :] for t in range(2)], axis=0)
            xh, xm, xl = parts(x, 3)
            columns.append(jnp.concatenate([xh, xm, xh, xm, xl, xh], axis=0))
        res = dot(left, jnp.concatenate(columns, axis=1))
        res = jnp.where(lane, res[:pairs], res[pairs:])
        tmp_ref[n * pairs : (n + 1) * pairs, :] = res[:, :128]
        tmp_ref[(n + 1) * pairs : (n + 2) * pairs, :] = res[:, 128:]
    squares = jnp.zeros((UNIT, 128), F32)
    for p in range(pairs):
        value = tmp_ref[pl.ds(p, UNIT, stride=pairs), :].astype(BF16)
        q_ref[mine, p * 128 : (p + 1) * 128] = value
        wide_value = value.astype(F32)
        squares = squares + wide_value * wide_value
    return squares


def kernel(
    g_hbm, s_hbm, left_hbm, right_hbm, ids_hbm, off_ref, out_ref,
    g_ref, s_ref, left_ref, right_ref, ids_ref, mid_ref, cond_ref, q_ref, p_ref, z_ref, ys_ref, yr_ref,
    nv_ref, nz_ref, ny_ref, nt_ref, nb_ref,
    load_sem, g_send, g_recv, z_send, z_recv, y_send, y_recv,
    nz_send, nz_recv, ny_send, ny_recv, nb_send, nb_recv,
):
    ex, lay = lax.axis_index("ex"), lax.axis_index("lay")
    core, x, yl = ex % 2, (ex // 2) % 4, ex // 8
    z, yh = lay % 8, lay // 8
    sibling = ex + 1 - 2 * core
    x_up = yl * 8 + ((x + 1) % 4) * 2 + core
    x_down = yl * 8 + ((x + 3) % 4) * 2 + core
    y_mate = (ex + 8) % 16
    examples = s_ref.shape[0]

    first = [
        pltpu.make_async_copy(src, dst, load_sem.at[4 + i])
        for i, (src, dst) in enumerate([(right_hbm, right_ref), (g_hbm, g_ref), (left_hbm, left_ref)])
    ]
    for copy in first:
        copy.start()

    barrier = pltpu.get_barrier_semaphore()
    for k in range(1, 16):
        pl.semaphore_signal(barrier, inc=1, device_id=((ex + k) % 16, lay), device_id_type=MESH)
    for k in range(1, 8):
        pl.semaphore_signal(barrier, inc=1, device_id=(ex, yh * 8 + (z + k) % 8), device_id_type=MESH)
    for k in range(1, 4):
        pl.semaphore_signal(barrier, inc=1, device_id=(ex, (lay + 8 * k) % 32), device_id_type=MESH)

    small = [pltpu.make_async_copy(ids_hbm, ids_ref, load_sem.at[7])]
    load_s = [
        pltpu.make_async_copy(s_hbm.at[pl.ds(128 * i, 128)], s_ref.at[pl.ds(128 * i, 128)], load_sem.at[i])
        for i in range(4)
    ]
    for copy in load_s + small:
        copy.start()
    nv_ref[...] = jnp.zeros_like(nv_ref)
    for copy in first:
        copy.wait()
    left, right_parts = factors(left_ref, right_ref, cond_ref.at[1])
    squares_1 = condition(g_ref, 1, left, right_parts, mid_ref.at[1], cond_ref.at[1], q_ref)

    pl.semaphore_wait(barrier, 25)

    width = q_ref.shape[1]

    def send(src, dst, to, part):
        span = pl.ds(0, width) if part is None else pl.ds(part * (width // 2), width // 2)
        pltpu.make_async_remote_copy(
            src_ref=q_ref.at[rows(src), span], dst_ref=q_ref.at[rows(dst), span], send_sem=g_send.at[0],
            recv_sem=g_recv.at[dst], device_id=(to, lay), device_id_type=MESH,
        ).start()

    def arrived(u):
        pltpu.make_async_copy(q_ref.at[rows(u)], q_ref.at[rows(u)], g_recv.at[u]).wait()

    def up(dx, dy, half, part=None):
        send(unit(dx, dy, 0, half), unit(dx - 1, dy, 0, half), x_up, part)

    def down(dx, dy, half, part=None):
        send(unit(dx, dy, 0, half), unit(dx + 1, dy, 0, half), x_down, part)

    def across(dx, dy, half, part=None):
        send(unit(dx, dy, 0, half), unit(dx, dy + 1, 0, half), y_mate, part)

    def share(dx, dy, half, part=None):
        send(unit(dx, dy, 0, half), unit(dx, dy, 1, half), sibling, part)

    def take(dx, dy, half):
        arrived(unit(dx, dy, 0, half))

    up(0, 0, 1)
    down(0, 0, 1)
    across(0, 0, 1)
    share(0, 0, 1)
    squares_0 = condition(g_ref, 0, left, right_parts, mid_ref.at[0], cond_ref.at[0], q_ref)
    across(0, 0, 0)
    up(0, 0, 0)
    down(0, 0, 0)
    share(0, 0, 0)
    squares = jnp.concatenate([squares_0, squares_1], axis=0)

    for copy in load_s + small:
        copy.wait()
    nv_ref[4:5, 0:32] = jnp.sum(squares.T, axis=0, keepdims=True)

    for block in range(4):
        pieces = []
        for part in range(2):
            total = jnp.zeros((64, 128), F32)
            for t in range(32):
                value = s_ref[block * 128 + part * 64 : block * 128 + part * 64 + 64, t * 128 : (t + 1) * 128].astype(F32)
                total = total + value * value
            pieces.append(total)
        nv_ref[block : block + 1, :] = jnp.sum(jnp.concatenate(pieces, axis=0).T, axis=0, keepdims=True)

    def z_norm(k):
        return pltpu.make_async_remote_copy(
            src_ref=nv_ref, dst_ref=nz_ref.at[k], send_sem=nz_send.at[k], recv_sem=nz_recv.at[k],
            device_id=(ex, yh * 8 + (z + k + 1) % 8), device_id_type=MESH,
        )

    for k in range(7):
        z_norm(k).start()

    def y_norm(k):
        return pltpu.make_async_remote_copy(
            src_ref=ny_ref.at[3], dst_ref=ny_ref.at[k], send_sem=ny_send.at[k], recv_sem=ny_recv.at[k],
            device_id=(ex, (lay + 8 * (k + 1)) % 32), device_id_type=MESH,
        )

    def b_norm(k):
        return pltpu.make_async_remote_copy(
            src_ref=nt_ref, dst_ref=nb_ref, send_sem=nb_send.at[k], recv_sem=nb_recv.at[0],
            device_id=((ex + k + 1) % 16, lay), device_id_type=MESH,
        )

    owner = lay // 2

    def norms_over_z():
        total = nv_ref[...]
        for k in range(7):
            z_norm(k).wait_recv()
            total = total + nz_ref[k]
        ny_ref[3] = total
        for k in range(3):
            y_norm(k).start()

    def norms_over_y():
        total = ny_ref[3]
        for k in range(3):
            y_norm(k).wait_recv()
            total = total + ny_ref[k]
        nt_ref[...] = total

        @pl.when(ex == owner)
        def _():
            for k in range(15):
                b_norm(k).start()

    def place(chip):
        dx, dy = CHIPS[chip]
        return (x + dx) % 4, (yl + dy) % 2

    def multiply(batch, cuts=1):
        first = PLACES.index(BATCHES[batch][0][:2] + (0,) + BATCHES[batch][0][2:])
        for dx, dy, half in BATCHES[batch]:
            arrived(unit(dx, dy, 1, half))
        span = rows(first, 2 * len(BATCHES[batch]))
        wide = examples // cuts
        for cut in range(cuts):
            columns = slice(cut * wide, (cut + 1) * wide)
            p_ref[span, columns] = dot(q_ref[span, :], s_ref[columns, :], NT).astype(BF16)
            for dx, dy, half in BATCHES[batch]:
                chip = CHIPS.index((dx, dy))
                for other in range(2):
                    u = unit(dx, dy, other, half)
                    goal = 4 * ((x + dx) % 2) + 2 * ((core + other) % 2) + half

                    @pl.when(goal != z)
                    def _():
                        pltpu.make_async_remote_copy(
                            src_ref=p_ref.at[rows(u), pl.ds(cut * wide, wide)],
                            dst_ref=z_ref.at[chip, (z + 8 - goal) % 8, :, pl.ds(cut * wide, wide)],
                            send_sem=z_send.at[chip], recv_sem=z_recv.at[chip],
                            device_id=(ex, yh * 8 + goal), device_id_type=MESH,
                        ).start()

                    @pl.when(goal == z)
                    def _():
                        z_ref[chip, 0, :, columns] = p_ref[rows(u), columns]

    def mine(chip):
        its_x, _ = place(chip)
        return its_x % 2 == z // 4

    def goal_of(chip):
        its_x, its_y = place(chip)
        return 2 * its_y + its_x // 2

    def y_copy(chip):
        goal = goal_of(chip)
        return pltpu.make_async_remote_copy(
            src_ref=ys_ref.at[chip], dst_ref=yr_ref.at[(yh + 4 - goal) % 4],
            send_sem=y_send.at[chip], recv_sem=y_recv.at[(yh + 4 - goal) % 4],
            device_id=(ex, goal * 8 + z), device_id_type=MESH,
        )

    def sum_over_z(dx, dy):
        chip = CHIPS.index((dx, dy))

        @pl.when(mine(chip))
        def _():
            pltpu.make_async_copy(
                z_ref.at[chip, pl.ds(1, 7)], z_ref.at[chip, pl.ds(1, 7)], z_recv.at[chip]
            ).wait()
            total = z_ref[chip, 0].astype(F32)
            for k in range(1, 8):
                total = total + z_ref[chip, k].astype(F32)
            goal = goal_of(chip)

            @pl.when(goal == yh)
            def _():
                yr_ref[0] = total

            @pl.when(goal != yh)
            def _():
                ys_ref[chip] = total
                y_copy(chip).start()

    multiply(0)

    take(3, 0, 1)
    take(1, 0, 1)

    @pl.when(core == 0)
    def _():
        up(3, 0, 1)
        across(1, 0, 1)
        across(3, 0, 1)

    @pl.when(core == 1)
    def _():
        down(1, 0, 1)
        across(3, 0, 1)
        across(1, 0, 1)

    share(3, 0, 1)
    share(1, 0, 1)
    take(0, 1, 1)
    share(0, 1, 1)

    take(0, 1, 0)
    up(0, 1, 0)
    down(0, 1, 0)
    share(0, 1, 0)
    take(3, 0, 0)
    take(1, 0, 0)

    @pl.when(core == 0)
    def _():
        down(1, 0, 0)

    @pl.when(core == 1)
    def _():
        up(3, 0, 0)

    share(3, 0, 0)
    share(1, 0, 0)
    norms_over_z()
    multiply(1)
    sum_over_z(0, 0)

    take(2, 0, 1)
    across(2, 0, 1, 1)
    share(2, 0, 1)

    @pl.when(core == 0)
    def _():
        take(1, 1, 1)
        down(1, 1, 1, 0)
        share(1, 1, 1)

    @pl.when(core == 1)
    def _():
        take(3, 1, 1)
        up(3, 1, 1, 0)
        share(3, 1, 1)

    take(3, 1, 0)
    take(1, 1, 0)

    @pl.when(core == 0)
    def _():
        up(3, 1, 0)

    @pl.when(core == 1)
    def _():
        down(1, 1, 0)

    share(3, 1, 0)
    share(1, 1, 0)
    take(2, 0, 0)
    share(2, 0, 0)

    @pl.when(core == 0)
    def _():
        take(3, 1, 1)
        share(3, 1, 1)

    @pl.when(core == 1)
    def _():
        take(1, 1, 1)
        share(1, 1, 1)

    norms_over_y()

    take(2, 1, 0)
    share(2, 1, 0)
    multiply(2)
    take(2, 1, 1)
    share(2, 1, 1)
    sum_over_z(0, 1)
    sum_over_z(1, 0)
    sum_over_z(3, 0)
    multiply(3, cuts=2)
    sum_over_z(2, 0)
    sum_over_z(1, 1)
    sum_over_z(3, 1)

    @pl.when(ex == owner)
    def _():
        nb_ref[...] = nt_ref[...]

    @pl.when(ex != owner)
    def _():
        b_norm(0).wait_recv()

    pltpu.make_async_copy(q_ref.at[rows(0, 30)], q_ref.at[rows(0, 30)], g_send.at[0]).wait()
    for k in range(7):
        z_norm(k).wait_send()
    for k in range(3):
        y_norm(k).wait_send()

    @pl.when(ex == owner)
    def _():
        for k in range(15):
            b_norm(k).wait_send()

    sum_over_z(2, 1)
    for chip in range(8):

        @pl.when(mine(chip))
        def _():
            pltpu.make_async_copy(p_ref.at[rows(0, 3)], p_ref.at[rows(0, 3)], z_send.at[chip]).wait()

        @pl.when(jnp.logical_not(mine(chip)))
        def _():
            pltpu.make_async_copy(p_ref.at[rows(0, 4)], p_ref.at[rows(0, 4)], z_send.at[chip]).wait()

    columns = nb_ref[...].T[:, 4:5]
    query_sq = jnp.where(lay % 2 == 0, columns[:UNIT], columns[UNIT : 2 * UNIT])
    query_scale = lax.rsqrt(query_sq + 1e-06)
    scale = jnp.sqrt(F32(SIDE * SIDE * 32))
    which = lax.broadcasted_iota(jnp.int32, (UNIT, 128), 0)
    ids = jnp.zeros((UNIT, 128), jnp.int32)
    for i in range(UNIT):
        ids = jnp.where(which == i, ids_ref[lay * UNIT + i], ids)
    place_of = lax.broadcasted_iota(jnp.int32, (UNIT, 128), 1) + off_ref[0]
    for k in range(1, 4):
        pltpu.make_async_copy(yr_ref.at[k], yr_ref.at[k], y_recv.at[k]).wait()
    for block in range(4):
        span = slice(block * 128, (block + 1) * 128)
        total = yr_ref[0, :, span] + yr_ref[1, :, span] + yr_ref[2, :, span] + yr_ref[3, :, span]
        example_scale = lax.rsqrt(nt_ref[block : block + 1, :] + 1e-06)
        value = total * query_scale * example_scale * scale
        out_ref[:, span] = jnp.where(ids == place_of + block * 128, F32(0.0), value)
    for chip in range(8):

        @pl.when(jnp.logical_and(mine(chip), goal_of(chip) != yh))
        def _():
            y_copy(chip).wait_send()


def per_device(query_grads, store, left_inv, right_inv, query_ids, block_offsets):
    count, _, width = query_grads.shape
    examples = store.shape[0]
    vmem = pl.BlockSpec(memory_space=pltpu.VMEM)
    hbm = pl.BlockSpec(memory_space=pltpu.HBM)
    dma = pltpu.SemaphoreType.DMA
    return pl.pallas_call(
        kernel,
        out_shape=pltpu.VMEM((UNIT, examples), F32),
        in_specs=[hbm] * 5 + [pl.BlockSpec(memory_space=pltpu.SMEM)],
        out_specs=vmem,
        scratch_shapes=[
            pltpu.VMEM((count, width), BF16),
            pltpu.VMEM((examples, width), BF16),
            pltpu.VMEM((SIDE, SIDE), F32),
            pltpu.VMEM((SIDE, SIDE), F32),
            pltpu.SMEM(query_ids.shape, jnp.int32),
            pltpu.VMEM((2, 2, 512, 128), F32),
            pltpu.VMEM((2, 512, 128), F32),
            pltpu.VMEM((512, width), BF16),
            pltpu.VMEM((512, examples), BF16),
            pltpu.VMEM((8, 8, UNIT, examples), BF16),
            pltpu.VMEM((8, UNIT, examples), F32),
            pltpu.VMEM((4, UNIT, examples), F32),
            pltpu.VMEM((8, 128), F32),
            pltpu.VMEM((7, 8, 128), F32),
            pltpu.VMEM((4, 8, 128), F32),
            pltpu.VMEM((8, 128), F32),
            pltpu.VMEM((8, 128), F32),
            dma((8,)),
            dma((1,)),
            dma((32,)),
            dma((8,)),
            dma((8,)),
            dma((8,)),
            dma((4,)),
            dma((7,)),
            dma((7,)),
            dma((3,)),
            dma((3,)),
            dma((15,)),
            dma((1,)),
        ],
        compiler_params=pltpu.CompilerParams(
            collective_id=0, has_side_effects=True, vmem_limit_bytes=60 * 2**20
        ),
        cost_estimate=pl.CostEstimate(
            flops=2 * 512 * examples * width, bytes_accessed=(examples + count) * width * 2, transcendentals=0
        ),
    )(
        query_grads.reshape(count, width),
        store.reshape(examples, width),
        left_inv.reshape(SIDE, SIDE),
        right_inv.reshape(SIDE, SIDE),
        query_ids,
        block_offsets,
    )


def solution(mesh):
    return jax.shard_map(
        per_device,
        mesh=mesh,
        in_specs=(
            P("ex", "lay", None),
            P("ex", "lay", None),
            P("lay", None, None),
            P("lay", None, None),
            P(),
            P("ex"),
        ),
        out_specs=P("lay", "ex"),
        check_vma=False,
    )
```

```python
import functools

import jax
import jax.numpy as jnp
from jax import lax
from jax.experimental import pallas as pl
from jax.experimental.pallas import tpu as pltpu
from jax.sharding import PartitionSpec as P

F32, BF16 = jnp.float32, jnp.bfloat16
MESH = pl.DeviceIdType.MESH
NT = (((1,), (1,)), ((), ()))
NN = (((1,), (0,)), ((), ()))

CHIPS = [(0, 0), (0, 1), (1, 0), (3, 0), (2, 0), (1, 1), (3, 1), (2, 1)]
BATCHES = [
    [(0, 0, 0), (0, 0, 1)],
    [(1, 0, 1), (3, 0, 1), (0, 1, 1), (1, 0, 0), (3, 0, 0), (0, 1, 0)],
    [(2, 0, 1), (1, 1, 0), (3, 1, 0), (2, 0, 0), (1, 1, 1), (3, 1, 1)],
    [(2, 1, 0), (2, 1, 1)],
]
PLACES = [
    (dx, dy, other, half) for batch in BATCHES for other in range(2) for dx, dy, half in batch
]
UNIT = 16
SIDE = 64


def unit(dx, dy, other, half):
    return PLACES.index((dx % 4, dy % 2, other, half))


def rows(u, n=1):
    return pl.ds(u * UNIT, n * UNIT)


def parts(value, n):
    out = []
    for _ in range(n):
        top = value.astype(BF16)
        out.append(top)
        value = value - top.astype(F32)
    return out


def dot(a, b, dims=NN):
    return lax.dot_general(a, b, dims, preferred_element_type=F32)


def factors(left_ref, right_ref, tmp_ref):
    pairs = SIDE // 2
    right = right_ref[...]
    wide = jnp.concatenate([right, right], axis=1)
    tall = jnp.concatenate([wide, wide], axis=0)
    row = lax.broadcasted_iota(jnp.int32, tall.shape, 0) < SIDE
    lane = lax.broadcasted_iota(jnp.int32, tall.shape, 1) < SIDE
    same = jnp.where(row == lane, tall, 0.0)
    cross = jnp.where(row == lane, 0.0, tall)
    right_parts = parts(jnp.concatenate([same, cross], axis=1), 3)

    pick_r = lax.broadcasted_iota(jnp.int32, (SIDE, SIDE), 0)
    pick_c = lax.broadcasted_iota(jnp.int32, (SIDE, SIDE), 1)
    even_odd = jnp.where(pick_c < pairs, 2 * pick_c, 2 * (pick_c - pairs) + 1)
    odd_even = jnp.where(pick_c < pairs, 2 * pick_c + 1, 2 * (pick_c - pairs))
    to_eo = jnp.where(pick_r == even_odd, 1.0, 0.0).astype(BF16)
    to_oe = jnp.where(pick_r == odd_even, 1.0, 0.0).astype(BF16)
    tmp_ref[0:SIDE, :] = jnp.concatenate([left_ref[...], jnp.zeros((SIDE, SIDE), F32)], axis=1)
    even_rows = parts(tmp_ref[pl.ds(0, pairs, stride=2), :][:, :SIDE], 3)
    odd_rows = parts(tmp_ref[pl.ds(1, pairs, stride=2), :][:, :SIDE], 3)
    high, middle, low = [
        jnp.concatenate([dot(e, to_eo), dot(o, to_oe)], axis=0).astype(BF16)
        for e, o in zip(even_rows, odd_rows)
    ]
    left = jnp.concatenate([high, high, middle, middle, high, low], axis=1)
    return left, right_parts


def condition(g_ref, half, left, right_parts, mid_ref, tmp_ref, q_ref):
    pairs = SIDE // 2
    mine = slice(half * UNIT, (half + 1) * UNIT)
    grads = jnp.concatenate([g_ref[mine, p * 128 : (p + 1) * 128] for p in range(pairs)], axis=0)
    total = None
    for part in right_parts:
        term = dot(grads, part)
        total = term if total is None else total + term
    mid_ref[0] = total[:, :128]
    mid_ref[1] = total[:, 128:]
    lane = lax.broadcasted_iota(jnp.int32, (pairs, 256), 1) % 128 < SIDE
    for n in range(0, UNIT, 2):
        columns = []
        for i in (n, n + 1):
            x = jnp.concatenate([mid_ref[t, pl.ds(i, pairs, stride=UNIT), :] for t in range(2)], axis=0)
            xh, xm, xl = parts(x, 3)
            columns.append(jnp.concatenate([xh, xm, xh, xm, xl, xh], axis=0))
        res = dot(left, jnp.concatenate(columns, axis=1))
        res = jnp.where(lane, res[:pairs], res[pairs:])
        tmp_ref[n * pairs : (n + 1) * pairs, :] = res[:, :128]
        tmp_ref[(n + 1) * pairs : (n + 2) * pairs, :] = res[:, 128:]
    squares = jnp.zeros((UNIT, 128), F32)
    for p in range(pairs):
        value = tmp_ref[pl.ds(p, UNIT, stride=pairs), :].astype(BF16)
        q_ref[mine, p * 128 : (p + 1) * 128] = value
        wide_value = value.astype(F32)
        squares = squares + wide_value * wide_value
    return squares


def kernel(
    g_hbm, s_hbm, left_hbm, right_hbm, ids_hbm, off_ref, out_ref,
    g_ref, s_ref, left_ref, right_ref, ids_ref, mid_ref, cond_ref, q_ref, p_ref, z_ref, ys_ref, yr_ref,
    nv_ref, nz_ref, ny_ref, nt_ref, nb_ref,
    load_sem, g_send, g_recv, z_send, z_recv, y_send, y_recv,
    nz_send, nz_recv, ny_send, ny_recv, nb_send, nb_recv,
):
    ex, lay = lax.axis_index("ex"), lax.axis_index("lay")
    core, x, yl = ex % 2, (ex // 2) % 4, ex // 8
    z, yh = lay % 8, lay // 8
    sibling = ex + 1 - 2 * core
    x_up = yl * 8 + ((x + 1) % 4) * 2 + core
    x_down = yl * 8 + ((x + 3) % 4) * 2 + core
    y_mate = (ex + 8) % 16
    examples = s_ref.shape[0]

    first = [
        pltpu.make_async_copy(src, dst, load_sem.at[4 + i])
        for i, (src, dst) in enumerate([(right_hbm, right_ref), (g_hbm, g_ref), (left_hbm, left_ref)])
    ]
    for copy in first:
        copy.start()

    barrier = pltpu.get_barrier_semaphore()
    for k in range(1, 16):
        pl.semaphore_signal(barrier, inc=1, device_id=((ex + k) % 16, lay), device_id_type=MESH)
    for k in range(1, 8):
        pl.semaphore_signal(barrier, inc=1, device_id=(ex, yh * 8 + (z + k) % 8), device_id_type=MESH)
    for k in range(1, 4):
        pl.semaphore_signal(barrier, inc=1, device_id=(ex, (lay + 8 * k) % 32), device_id_type=MESH)

    small = [pltpu.make_async_copy(ids_hbm, ids_ref, load_sem.at[7])]
    load_s = [
        pltpu.make_async_copy(s_hbm.at[pl.ds(128 * i, 128)], s_ref.at[pl.ds(128 * i, 128)], load_sem.at[i])
        for i in range(4)
    ]
    for copy in load_s + small:
        copy.start()
    nv_ref[...] = jnp.zeros_like(nv_ref)
    first[0].wait()
    first[2].wait()
    left, right_parts = factors(left_ref, right_ref, cond_ref.at[1])
    first[1].wait()
    squares_1 = condition(g_ref, 1, left, right_parts, mid_ref.at[1], cond_ref.at[1], q_ref)

    pl.semaphore_wait(barrier, 25)

    width = q_ref.shape[1]

    def send(src, dst, to, part):
        span = pl.ds(0, width) if part is None else pl.ds(part * (width // 2), width // 2)
        pltpu.make_async_remote_copy(
            src_ref=q_ref.at[rows(src), span], dst_ref=q_ref.at[rows(dst), span], send_sem=g_send.at[0],
            recv_sem=g_recv.at[dst], device_id=(to, lay), device_id_type=MESH,
        ).start()

    def arrived(u):
        pltpu.make_async_copy(q_ref.at[rows(u)], q_ref.at[rows(u)], g_recv.at[u]).wait()

    def up(dx, dy, half, part=None):
        send(unit(dx, dy, 0, half), unit(dx - 1, dy, 0, half), x_up, part)

    def down(dx, dy, half, part=None):
        send(unit(dx, dy, 0, half), unit(dx + 1, dy, 0, half), x_down, part)

    def across(dx, dy, half, part=None):
        send(unit(dx, dy, 0, half), unit(dx, dy + 1, 0, half), y_mate, part)

    def share(dx, dy, half, part=None):
        send(unit(dx, dy, 0, half), unit(dx, dy, 1, half), sibling, part)

    def take(dx, dy, half):
        arrived(unit(dx, dy, 0, half))

    up(0, 0, 1)
    down(0, 0, 1)
    across(0, 0, 1)
    share(0, 0, 1)
    squares_0 = condition(g_ref, 0, left, right_parts, mid_ref.at[0], cond_ref.at[0], q_ref)
    across(0, 0, 0)
    up(0, 0, 0)
    down(0, 0, 0)
    share(0, 0, 0)
    squares = jnp.concatenate([squares_0, squares_1], axis=0)

    for copy in load_s + small:
        copy.wait()
    nv_ref[4:5, 0:32] = jnp.sum(squares.T, axis=0, keepdims=True)

    for block in range(4):
        pieces = []
        for part in range(2):
            total = jnp.zeros((64, 128), F32)
            for t in range(32):
                value = s_ref[block * 128 + part * 64 : block * 128 + part * 64 + 64, t * 128 : (t + 1) * 128].astype(F32)
                total = total + value * value
            pieces.append(total)
        nv_ref[block : block + 1, :] = jnp.sum(jnp.concatenate(pieces, axis=0).T, axis=0, keepdims=True)

    def z_norm(k):
        return pltpu.make_async_remote_copy(
            src_ref=nv_ref, dst_ref=nz_ref.at[k], send_sem=nz_send.at[k], recv_sem=nz_recv.at[k],
            device_id=(ex, yh * 8 + (z + k + 1) % 8), device_id_type=MESH,
        )

    for k in range(7):
        z_norm(k).start()

    def y_norm(k):
        return pltpu.make_async_remote_copy(
            src_ref=ny_ref.at[3], dst_ref=ny_ref.at[k], send_sem=ny_send.at[k], recv_sem=ny_recv.at[k],
            device_id=(ex, (lay + 8 * (k + 1)) % 32), device_id_type=MESH,
        )

    def b_norm(k):
        return pltpu.make_async_remote_copy(
            src_ref=nt_ref, dst_ref=nb_ref, send_sem=nb_send.at[k], recv_sem=nb_recv.at[0],
            device_id=((ex + k + 1) % 16, lay), device_id_type=MESH,
        )

    owner = lay // 2

    def norms_over_z():
        total = nv_ref[...]
        for k in range(7):
            z_norm(k).wait_recv()
            total = total + nz_ref[k]
        ny_ref[3] = total
        for k in range(3):
            y_norm(k).start()

    def norms_over_y():
        total = ny_ref[3]
        for k in range(3):
            y_norm(k).wait_recv()
            total = total + ny_ref[k]
        nt_ref[...] = total

        @pl.when(ex == owner)
        def _():
            for k in range(15):
                b_norm(k).start()

    def place(chip):
        dx, dy = CHIPS[chip]
        return (x + dx) % 4, (yl + dy) % 2

    def multiply(batch, cuts=1):
        first = PLACES.index(BATCHES[batch][0][:2] + (0,) + BATCHES[batch][0][2:])
        for dx, dy, half in BATCHES[batch]:
            arrived(unit(dx, dy, 1, half))
        span = rows(first, 2 * len(BATCHES[batch]))
        wide = examples // cuts
        for cut in range(cuts):
            columns = slice(cut * wide, (cut + 1) * wide)
            p_ref[span, columns] = dot(q_ref[span, :], s_ref[columns, :], NT).astype(BF16)
            for dx, dy, half in BATCHES[batch]:
                chip = CHIPS.index((dx, dy))
                for other in range(2):
                    u = unit(dx, dy, other, half)
                    goal = 4 * ((x + dx) % 2) + 2 * ((core + other) % 2) + half

                    @pl.when(goal != z)
                    def _():
                        pltpu.make_async_remote_copy(
                            src_ref=p_ref.at[rows(u), pl.ds(cut * wide, wide)],
                            dst_ref=z_ref.at[chip, (z + 8 - goal) % 8, :, pl.ds(cut * wide, wide)],
                            send_sem=z_send.at[chip], recv_sem=z_recv.at[chip],
                            device_id=(ex, yh * 8 + goal), device_id_type=MESH,
                        ).start()

                    @pl.when(goal == z)
                    def _():
                        z_ref[chip, 0, :, columns] = p_ref[rows(u), columns]

    def mine(chip):
        its_x, _ = place(chip)
        return its_x % 2 == z // 4

    def goal_of(chip):
        its_x, its_y = place(chip)
        return 2 * its_y + its_x // 2

    def y_copy(chip):
        goal = goal_of(chip)
        return pltpu.make_async_remote_copy(
            src_ref=ys_ref.at[chip], dst_ref=yr_ref.at[(yh + 4 - goal) % 4],
            send_sem=y_send.at[chip], recv_sem=y_recv.at[(yh + 4 - goal) % 4],
            device_id=(ex, goal * 8 + z), device_id_type=MESH,
        )

    def sum_over_z(dx, dy):
        chip = CHIPS.index((dx, dy))

        @pl.when(mine(chip))
        def _():
            pltpu.make_async_copy(
                z_ref.at[chip, pl.ds(1, 7)], z_ref.at[chip, pl.ds(1, 7)], z_recv.at[chip]
            ).wait()
            total = z_ref[chip, 0].astype(F32)
            for k in range(1, 8):
                total = total + z_ref[chip, k].astype(F32)
            goal = goal_of(chip)

            @pl.when(goal == yh)
            def _():
                yr_ref[0] = total

            @pl.when(goal != yh)
            def _():
                ys_ref[chip] = total
                y_copy(chip).start()

    multiply(0)

    take(3, 0, 1)
    take(1, 0, 1)

    @pl.when(core == 0)
    def _():
        up(3, 0, 1)
        across(1, 0, 1)
        across(3, 0, 1)

    @pl.when(core == 1)
    def _():
        down(1, 0, 1)
        across(3, 0, 1)
        across(1, 0, 1)

    share(3, 0, 1)
    share(1, 0, 1)
    take(0, 1, 1)
    share(0, 1, 1)

    take(0, 1, 0)
    up(0, 1, 0)
    down(0, 1, 0)
    share(0, 1, 0)
    take(3, 0, 0)
    take(1, 0, 0)

    @pl.when(core == 0)
    def _():
        down(1, 0, 0)

    @pl.when(core == 1)
    def _():
        up(3, 0, 0)

    share(3, 0, 0)
    share(1, 0, 0)
    norms_over_z()
    multiply(1)
    sum_over_z(0, 0)

    take(2, 0, 1)
    across(2, 0, 1, 1)
    share(2, 0, 1)

    @pl.when(core == 0)
    def _():
        take(1, 1, 1)
        down(1, 1, 1, 0)
        share(1, 1, 1)

    @pl.when(core == 1)
    def _():
        take(3, 1, 1)
        up(3, 1, 1, 0)
        share(3, 1, 1)

    take(3, 1, 0)
    take(1, 1, 0)

    @pl.when(core == 0)
    def _():
        up(3, 1, 0)

    @pl.when(core == 1)
    def _():
        down(1, 1, 0)

    share(3, 1, 0)
    share(1, 1, 0)
    take(2, 0, 0)
    share(2, 0, 0)

    @pl.when(core == 0)
    def _():
        take(3, 1, 1)
        share(3, 1, 1)

    @pl.when(core == 1)
    def _():
        take(1, 1, 1)
        share(1, 1, 1)

    norms_over_y()

    take(2, 1, 0)
    share(2, 1, 0)
    multiply(2)
    take(2, 1, 1)
    share(2, 1, 1)
    sum_over_z(0, 1)
    sum_over_z(1, 0)
    sum_over_z(3, 0)
    multiply(3)
    sum_over_z(2, 0)
    sum_over_z(1, 1)
    sum_over_z(3, 1)

    @pl.when(ex == owner)
    def _():
        nb_ref[...] = nt_ref[...]

    @pl.when(ex != owner)
    def _():
        b_norm(0).wait_recv()

    pltpu.make_async_copy(q_ref.at[rows(0, 30)], q_ref.at[rows(0, 30)], g_send.at[0]).wait()
    for k in range(7):
        z_norm(k).wait_send()
    for k in range(3):
        y_norm(k).wait_send()

    @pl.when(ex == owner)
    def _():
        for k in range(15):
            b_norm(k).wait_send()

    sum_over_z(2, 1)
    for chip in range(8):

        @pl.when(mine(chip))
        def _():
            pltpu.make_async_copy(p_ref.at[rows(0, 3)], p_ref.at[rows(0, 3)], z_send.at[chip]).wait()

        @pl.when(jnp.logical_not(mine(chip)))
        def _():
            pltpu.make_async_copy(p_ref.at[rows(0, 4)], p_ref.at[rows(0, 4)], z_send.at[chip]).wait()

    columns = nb_ref[...].T[:, 4:5]
    query_sq = jnp.where(lay % 2 == 0, columns[:UNIT], columns[UNIT : 2 * UNIT])
    query_scale = lax.rsqrt(query_sq + 1e-06)
    scale = jnp.sqrt(F32(SIDE * SIDE * 32))
    which = lax.broadcasted_iota(jnp.int32, (UNIT, 128), 0)
    ids = jnp.zeros((UNIT, 128), jnp.int32)
    for i in range(UNIT):
        ids = jnp.where(which == i, ids_ref[lay * UNIT + i], ids)
    place_of = lax.broadcasted_iota(jnp.int32, (UNIT, 128), 1) + off_ref[0]
    for k in range(1, 4):
        pltpu.make_async_copy(yr_ref.at[k], yr_ref.at[k], y_recv.at[k]).wait()
    for block in range(4):
        span = slice(block * 128, (block + 1) * 128)
        total = yr_ref[0, :, span] + yr_ref[1, :, span] + yr_ref[2, :, span] + yr_ref[3, :, span]
        example_scale = lax.rsqrt(nt_ref[block : block + 1, :] + 1e-06)
        value = total * query_scale * example_scale * scale
        out_ref[:, span] = jnp.where(ids == place_of + block * 128, F32(0.0), value)
    for chip in range(8):

        @pl.when(jnp.logical_and(mine(chip), goal_of(chip) != yh))
        def _():
            y_copy(chip).wait_send()


def per_device(query_grads, store, left_inv, right_inv, query_ids, block_offsets):
    count, _, width = query_grads.shape
    examples = store.shape[0]
    vmem = pl.BlockSpec(memory_space=pltpu.VMEM)
    hbm = pl.BlockSpec(memory_space=pltpu.HBM)
    dma = pltpu.SemaphoreType.DMA
    return pl.pallas_call(
        kernel,
        out_shape=pltpu.VMEM((UNIT, examples), F32),
        in_specs=[hbm] * 5 + [pl.BlockSpec(memory_space=pltpu.SMEM)],
        out_specs=vmem,
        scratch_shapes=[
            pltpu.VMEM((count, width), BF16),
            pltpu.VMEM((examples, width), BF16),
            pltpu.VMEM((SIDE, SIDE), F32),
            pltpu.VMEM((SIDE, SIDE), F32),
            pltpu.SMEM(query_ids.shape, jnp.int32),
            pltpu.VMEM((2, 2, 512, 128), F32),
            pltpu.VMEM((2, 512, 128), F32),
            pltpu.VMEM((512, width), BF16),
            pltpu.VMEM((512, examples), BF16),
            pltpu.VMEM((8, 8, UNIT, examples), BF16),
            pltpu.VMEM((8, UNIT, examples), F32),
            pltpu.VMEM((4, UNIT, examples), F32),
            pltpu.VMEM((8, 128), F32),
            pltpu.VMEM((7, 8, 128), F32),
            pltpu.VMEM((4, 8, 128), F32),
            pltpu.VMEM((8, 128), F32),
            pltpu.VMEM((8, 128), F32),
            dma((8,)),
            dma((1,)),
            dma((32,)),
            dma((8,)),
            dma((8,)),
            dma((8,)),
            dma((4,)),
            dma((7,)),
            dma((7,)),
            dma((3,)),
            dma((3,)),
            dma((15,)),
            dma((1,)),
        ],
        compiler_params=pltpu.CompilerParams(
            collective_id=0, has_side_effects=True, vmem_limit_bytes=60 * 2**20
        ),
        cost_estimate=pl.CostEstimate(
            flops=2 * 512 * examples * width, bytes_accessed=(examples + count) * width * 2, transcendentals=0
        ),
    )(
        query_grads.reshape(count, width),
        store.reshape(examples, width),
        left_inv.reshape(SIDE, SIDE),
        right_inv.reshape(SIDE, SIDE),
        query_ids,
        block_offsets,
    )


def solution(mesh):
    return jax.shard_map(
        per_device,
        mesh=mesh,
        in_specs=(
            P("ex", "lay", None),
            P("ex", "lay", None),
            P("lay", None, None),
            P("lay", None, None),
            P(),
            P("ex"),
        ),
        out_specs=P("lay", "ex"),
        check_vma=False,
    )
```

```python
import functools

import jax
import jax.numpy as jnp
from jax import lax
from jax.experimental import pallas as pl
from jax.experimental.pallas import tpu as pltpu
from jax.sharding import PartitionSpec as P

F32, BF16 = jnp.float32, jnp.bfloat16
MESH = pl.DeviceIdType.MESH
NT = (((1,), (1,)), ((), ()))
NN = (((1,), (0,)), ((), ()))

CHIPS = [(0, 0), (0, 1), (1, 0), (3, 0), (2, 0), (1, 1), (3, 1), (2, 1)]
BATCHES = [
    [(0, 0, 0), (0, 0, 1)],
    [(1, 0, 1), (3, 0, 1), (0, 1, 1), (1, 0, 0), (3, 0, 0), (0, 1, 0)],
    [(2, 0, 1), (1, 1, 0), (3, 1, 0), (2, 0, 0), (1, 1, 1), (3, 1, 1)],
    [(2, 1, 0), (2, 1, 1)],
]
PLACES = [
    (dx, dy, other, half) for batch in BATCHES for other in range(2) for dx, dy, half in batch
]
UNIT = 16
SIDE = 64


def unit(dx, dy, other, half):
    return PLACES.index((dx % 4, dy % 2, other, half))


def rows(u, n=1):
    return pl.ds(u * UNIT, n * UNIT)


def parts(value, n):
    out = []
    for _ in range(n):
        top = value.astype(BF16)
        out.append(top)
        value = value - top.astype(F32)
    return out


def dot(a, b, dims=NN):
    return lax.dot_general(a, b, dims, preferred_element_type=F32)


def factors(left_ref, right_ref, tmp_ref):
    pairs = SIDE // 2
    right = right_ref[...]
    wide = jnp.concatenate([right, right], axis=1)
    tall = jnp.concatenate([wide, wide], axis=0)
    row = lax.broadcasted_iota(jnp.int32, tall.shape, 0) < SIDE
    lane = lax.broadcasted_iota(jnp.int32, tall.shape, 1) < SIDE
    same = jnp.where(row == lane, tall, 0.0)
    cross = jnp.where(row == lane, 0.0, tall)
    right_parts = parts(jnp.concatenate([same, cross], axis=1), 3)

    pick_r = lax.broadcasted_iota(jnp.int32, (SIDE, SIDE), 0)
    pick_c = lax.broadcasted_iota(jnp.int32, (SIDE, SIDE), 1)
    even_odd = jnp.where(pick_c < pairs, 2 * pick_c, 2 * (pick_c - pairs) + 1)
    odd_even = jnp.where(pick_c < pairs, 2 * pick_c + 1, 2 * (pick_c - pairs))
    to_eo = jnp.where(pick_r == even_odd, 1.0, 0.0).astype(BF16)
    to_oe = jnp.where(pick_r == odd_even, 1.0, 0.0).astype(BF16)
    tmp_ref[0:SIDE, :] = jnp.concatenate([left_ref[...], jnp.zeros((SIDE, SIDE), F32)], axis=1)
    even_rows = parts(tmp_ref[pl.ds(0, pairs, stride=2), :][:, :SIDE], 3)
    odd_rows = parts(tmp_ref[pl.ds(1, pairs, stride=2), :][:, :SIDE], 3)
    high, middle, low = [
        jnp.concatenate([dot(e, to_eo), dot(o, to_oe)], axis=0).astype(BF16)
        for e, o in zip(even_rows, odd_rows)
    ]
    left = jnp.concatenate([high, high, middle, middle, high, low], axis=1)
    return left, right_parts


def condition(g_ref, half, left, right_parts, mid_ref, tmp_ref, q_ref):
    pairs = SIDE // 2
    mine = slice(half * UNIT, (half + 1) * UNIT)
    grads = jnp.concatenate([g_ref[mine, p * 128 : (p + 1) * 128] for p in range(pairs)], axis=0)
    total = None
    for part in right_parts:
        term = dot(grads, part)
        total = term if total is None else total + term
    mid_ref[0] = total[:, :128]
    mid_ref[1] = total[:, 128:]
    lane = lax.broadcasted_iota(jnp.int32, (pairs, 256), 1) % 128 < SIDE
    for n in range(0, UNIT, 2):
        columns = []
        for i in (n, n + 1):
            x = jnp.concatenate([mid_ref[t, pl.ds(i, pairs, stride=UNIT), :] for t in range(2)], axis=0)
            xh, xm, xl = parts(x, 3)
            columns.append(jnp.concatenate([xh, xm, xh, xm, xl, xh], axis=0))
        res = dot(left, jnp.concatenate(columns, axis=1))
        res = jnp.where(lane, res[:pairs], res[pairs:])
        tmp_ref[n * pairs : (n + 1) * pairs, :] = res[:, :128]
        tmp_ref[(n + 1) * pairs : (n + 2) * pairs, :] = res[:, 128:]
    squares = jnp.zeros((UNIT, 128), F32)
    for p in range(pairs):
        value = tmp_ref[pl.ds(p, UNIT, stride=pairs), :].astype(BF16)
        q_ref[mine, p * 128 : (p + 1) * 128] = value
        wide_value = value.astype(F32)
        squares = squares + wide_value * wide_value
    return squares


def kernel(
    g_hbm, s_hbm, left_hbm, right_hbm, ids_hbm, off_ref, out_ref,
    g_ref, s_ref, left_ref, right_ref, ids_ref, mid_ref, cond_ref, q_ref, p_ref, z_ref, ys_ref, yr_ref,
    nv_ref, nz_ref, ny_ref, nt_ref, nb_ref,
    load_sem, g_send, g_recv, z_send, z_recv, y_send, y_recv,
    nz_send, nz_recv, ny_send, ny_recv, nb_send, nb_recv,
):
    ex, lay = lax.axis_index("ex"), lax.axis_index("lay")
    core, x, yl = ex % 2, (ex // 2) % 4, ex // 8
    z, yh = lay % 8, lay // 8
    sibling = ex + 1 - 2 * core
    x_up = yl * 8 + ((x + 1) % 4) * 2 + core
    x_down = yl * 8 + ((x + 3) % 4) * 2 + core
    y_mate = (ex + 8) % 16
    examples = s_ref.shape[0]

    first = [
        pltpu.make_async_copy(src, dst, load_sem.at[4 + i])
        for i, (src, dst) in enumerate([(right_hbm, right_ref), (g_hbm, g_ref), (left_hbm, left_ref)])
    ]
    for copy in first:
        copy.start()

    barrier = pltpu.get_barrier_semaphore()
    for k in range(1, 16):
        pl.semaphore_signal(barrier, inc=1, device_id=((ex + k) % 16, lay), device_id_type=MESH)
    for k in range(1, 8):
        pl.semaphore_signal(barrier, inc=1, device_id=(ex, yh * 8 + (z + k) % 8), device_id_type=MESH)
    for k in range(1, 4):
        pl.semaphore_signal(barrier, inc=1, device_id=(ex, (lay + 8 * k) % 32), device_id_type=MESH)

    small = [pltpu.make_async_copy(ids_hbm, ids_ref, load_sem.at[7])]
    load_s = [
        pltpu.make_async_copy(s_hbm.at[pl.ds(128 * i, 128)], s_ref.at[pl.ds(128 * i, 128)], load_sem.at[i])
        for i in range(4)
    ]
    for copy in load_s + small:
        copy.start()
    nv_ref[...] = jnp.zeros_like(nv_ref)
    first[0].wait()
    first[2].wait()
    left, right_parts = factors(left_ref, right_ref, cond_ref.at[1])
    first[1].wait()
    squares_1 = condition(g_ref, 1, left, right_parts, mid_ref.at[1], cond_ref.at[1], q_ref)

    pl.semaphore_wait(barrier, 25)

    width = q_ref.shape[1]

    def send(src, dst, to, part):
        span = pl.ds(0, width) if part is None else pl.ds(part * (width // 2), width // 2)
        pltpu.make_async_remote_copy(
            src_ref=q_ref.at[rows(src), span], dst_ref=q_ref.at[rows(dst), span], send_sem=g_send.at[0],
            recv_sem=g_recv.at[dst], device_id=(to, lay), device_id_type=MESH,
        ).start()

    def arrived(u):
        pltpu.make_async_copy(q_ref.at[rows(u)], q_ref.at[rows(u)], g_recv.at[u]).wait()

    def up(dx, dy, half, part=None):
        send(unit(dx, dy, 0, half), unit(dx - 1, dy, 0, half), x_up, part)

    def down(dx, dy, half, part=None):
        send(unit(dx, dy, 0, half), unit(dx + 1, dy, 0, half), x_down, part)

    def across(dx, dy, half, part=None):
        send(unit(dx, dy, 0, half), unit(dx, dy + 1, 0, half), y_mate, part)

    def share(dx, dy, half, part=None):
        send(unit(dx, dy, 0, half), unit(dx, dy, 1, half), sibling, part)

    def take(dx, dy, half):
        arrived(unit(dx, dy, 0, half))

    up(0, 0, 1)
    down(0, 0, 1)
    across(0, 0, 1)
    share(0, 0, 1)
    squares_0 = condition(g_ref, 0, left, right_parts, mid_ref.at[0], cond_ref.at[0], q_ref)
    across(0, 0, 0)
    up(0, 0, 0)
    down(0, 0, 0)
    share(0, 0, 0)
    squares = jnp.concatenate([squares_0, squares_1], axis=0)

    for copy in load_s + small:
        copy.wait()
    nv_ref[4:5, 0:32] = jnp.sum(squares.T, axis=0, keepdims=True)

    for block in range(4):
        pieces = []
        for part in range(2):
            total = jnp.zeros((64, 128), F32)
            for t in range(32):
                value = s_ref[block * 128 + part * 64 : block * 128 + part * 64 + 64, t * 128 : (t + 1) * 128].astype(F32)
                total = total + value * value
            pieces.append(total)
        nv_ref[block : block + 1, :] = jnp.sum(jnp.concatenate(pieces, axis=0).T, axis=0, keepdims=True)

    def z_norm(k):
        return pltpu.make_async_remote_copy(
            src_ref=nv_ref, dst_ref=nz_ref.at[k], send_sem=nz_send.at[k], recv_sem=nz_recv.at[k],
            device_id=(ex, yh * 8 + (z + k + 1) % 8), device_id_type=MESH,
        )

    for k in range(7):
        z_norm(k).start()

    def y_norm(k):
        return pltpu.make_async_remote_copy(
            src_ref=ny_ref.at[3], dst_ref=ny_ref.at[k], send_sem=ny_send.at[k], recv_sem=ny_recv.at[k],
            device_id=(ex, (lay + 8 * (k + 1)) % 32), device_id_type=MESH,
        )

    def b_norm(k):
        return pltpu.make_async_remote_copy(
            src_ref=nt_ref, dst_ref=nb_ref, send_sem=nb_send.at[k], recv_sem=nb_recv.at[0],
            device_id=((ex + k + 1) % 16, lay), device_id_type=MESH,
        )

    owner = lay // 2

    def norms_over_z():
        total = nv_ref[...]
        for k in range(7):
            z_norm(k).wait_recv()
            total = total + nz_ref[k]
        ny_ref[3] = total
        for k in range(3):
            y_norm(k).start()

    def norms_over_y():
        total = ny_ref[3]
        for k in range(3):
            y_norm(k).wait_recv()
            total = total + ny_ref[k]
        nt_ref[...] = total

        @pl.when(ex == owner)
        def _():
            for k in range(15):
                b_norm(k).start()

    def place(chip):
        dx, dy = CHIPS[chip]
        return (x + dx) % 4, (yl + dy) % 2

    def multiply(batch, cuts=1):
        first = PLACES.index(BATCHES[batch][0][:2] + (0,) + BATCHES[batch][0][2:])
        for dx, dy, half in BATCHES[batch]:
            arrived(unit(dx, dy, 1, half))
        span = rows(first, 2 * len(BATCHES[batch]))
        wide = examples // cuts
        for cut in range(cuts):
            columns = slice(cut * wide, (cut + 1) * wide)
            p_ref[span, columns] = dot(q_ref[span, :], s_ref[columns, :], NT).astype(BF16)
            for dx, dy, half in BATCHES[batch]:
                chip = CHIPS.index((dx, dy))
                for other in range(2):
                    u = unit(dx, dy, other, half)
                    goal = 4 * ((x + dx) % 2) + 2 * ((core + other) % 2) + half

                    @pl.when(goal != z)
                    def _():
                        pltpu.make_async_remote_copy(
                            src_ref=p_ref.at[rows(u), pl.ds(cut * wide, wide)],
                            dst_ref=z_ref.at[chip, (z + 8 - goal) % 8, :, pl.ds(cut * wide, wide)],
                            send_sem=z_send.at[chip], recv_sem=z_recv.at[chip],
                            device_id=(ex, yh * 8 + goal), device_id_type=MESH,
                        ).start()

                    @pl.when(goal == z)
                    def _():
                        z_ref[chip, 0, :, columns] = p_ref[rows(u), columns]

    def mine(chip):
        its_x, _ = place(chip)
        return its_x % 2 == z // 4

    def goal_of(chip):
        its_x, its_y = place(chip)
        return 2 * its_y + its_x // 2

    def y_copy(chip):
        goal = goal_of(chip)
        return pltpu.make_async_remote_copy(
            src_ref=ys_ref.at[chip], dst_ref=yr_ref.at[(yh + 4 - goal) % 4],
            send_sem=y_send.at[chip], recv_sem=y_recv.at[(yh + 4 - goal) % 4],
            device_id=(ex, goal * 8 + z), device_id_type=MESH,
        )

    def sum_over_z(dx, dy):
        chip = CHIPS.index((dx, dy))

        @pl.when(mine(chip))
        def _():
            pltpu.make_async_copy(
                z_ref.at[chip, pl.ds(1, 7)], z_ref.at[chip, pl.ds(1, 7)], z_recv.at[chip]
            ).wait()
            total = z_ref[chip, 0].astype(F32)
            for k in range(1, 8):
                total = total + z_ref[chip, k].astype(F32)
            goal = goal_of(chip)

            @pl.when(goal == yh)
            def _():
                yr_ref[0] = total

            @pl.when(goal != yh)
            def _():
                ys_ref[chip] = total
                y_copy(chip).start()

    multiply(0)

    take(3, 0, 1)
    take(1, 0, 1)

    @pl.when(core == 0)
    def _():
        up(3, 0, 1)
        across(1, 0, 1)
        across(3, 0, 1)

    @pl.when(core == 1)
    def _():
        down(1, 0, 1)
        across(3, 0, 1)
        across(1, 0, 1)

    share(3, 0, 1)
    share(1, 0, 1)
    take(0, 1, 1)
    share(0, 1, 1)

    take(0, 1, 0)
    up(0, 1, 0)
    down(0, 1, 0)
    share(0, 1, 0)
    @pl.when(core == 0)
    def _():
        take(1, 0, 0)
        down(1, 0, 0)
        share(1, 0, 0)
        take(3, 0, 0)
        share(3, 0, 0)

    @pl.when(core == 1)
    def _():
        take(3, 0, 0)
        up(3, 0, 0)
        share(3, 0, 0)
        take(1, 0, 0)
        share(1, 0, 0)

    norms_over_z()
    multiply(1)
    sum_over_z(0, 0)

    take(2, 0, 1)
    across(2, 0, 1, 1)
    share(2, 0, 1)

    @pl.when(core == 0)
    def _():
        take(1, 1, 1)
        down(1, 1, 1, 0)
        share(1, 1, 1)

    @pl.when(core == 1)
    def _():
        take(3, 1, 1)
        up(3, 1, 1, 0)
        share(3, 1, 1)

    @pl.when(core == 0)
    def _():
        take(3, 1, 0)
        up(3, 1, 0)
        share(3, 1, 0)
        take(1, 1, 0)
        share(1, 1, 0)

    @pl.when(core == 1)
    def _():
        take(1, 1, 0)
        down(1, 1, 0)
        share(1, 1, 0)
        take(3, 1, 0)
        share(3, 1, 0)

    take(2, 0, 0)
    share(2, 0, 0)

    @pl.when(core == 0)
    def _():
        take(3, 1, 1)
        share(3, 1, 1)

    @pl.when(core == 1)
    def _():
        take(1, 1, 1)
        share(1, 1, 1)

    norms_over_y()

    take(2, 1, 0)
    share(2, 1, 0)
    multiply(2)
    take(2, 1, 1)
    share(2, 1, 1)
    sum_over_z(0, 1)
    sum_over_z(1, 0)
    sum_over_z(3, 0)
    multiply(3)
    sum_over_z(2, 0)
    sum_over_z(1, 1)
    sum_over_z(3, 1)

    @pl.when(ex == owner)
    def _():
        nb_ref[...] = nt_ref[...]

    @pl.when(ex != owner)
    def _():
        b_norm(0).wait_recv()

    pltpu.make_async_copy(q_ref.at[rows(0, 30)], q_ref.at[rows(0, 30)], g_send.at[0]).wait()
    for k in range(7):
        z_norm(k).wait_send()
    for k in range(3):
        y_norm(k).wait_send()

    @pl.when(ex == owner)
    def _():
        for k in range(15):
            b_norm(k).wait_send()

    sum_over_z(2, 1)
    for chip in range(8):

        @pl.when(mine(chip))
        def _():
            pltpu.make_async_copy(p_ref.at[rows(0, 3)], p_ref.at[rows(0, 3)], z_send.at[chip]).wait()

        @pl.when(jnp.logical_not(mine(chip)))
        def _():
            pltpu.make_async_copy(p_ref.at[rows(0, 4)], p_ref.at[rows(0, 4)], z_send.at[chip]).wait()

    columns = nb_ref[...].T[:, 4:5]
    query_sq = jnp.where(lay % 2 == 0, columns[:UNIT], columns[UNIT : 2 * UNIT])
    query_scale = lax.rsqrt(query_sq + 1e-06)
    scale = jnp.sqrt(F32(SIDE * SIDE * 32))
    which = lax.broadcasted_iota(jnp.int32, (UNIT, 128), 0)
    ids = jnp.zeros((UNIT, 128), jnp.int32)
    for i in range(UNIT):
        ids = jnp.where(which == i, ids_ref[lay * UNIT + i], ids)
    place_of = lax.broadcasted_iota(jnp.int32, (UNIT, 128), 1) + off_ref[0]
    for k in range(1, 4):
        pltpu.make_async_copy(yr_ref.at[k], yr_ref.at[k], y_recv.at[k]).wait()
    for block in range(4):
        span = slice(block * 128, (block + 1) * 128)
        total = yr_ref[0, :, span] + yr_ref[1, :, span] + yr_ref[2, :, span] + yr_ref[3, :, span]
        example_scale = lax.rsqrt(nt_ref[block : block + 1, :] + 1e-06)
        value = total * query_scale * example_scale * scale
        out_ref[:, span] = jnp.where(ids == place_of + block * 128, F32(0.0), value)
    for chip in range(8):

        @pl.when(jnp.logical_and(mine(chip), goal_of(chip) != yh))
        def _():
            y_copy(chip).wait_send()


def per_device(query_grads, store, left_inv, right_inv, query_ids, block_offsets):
    count, _, width = query_grads.shape
    examples = store.shape[0]
    vmem = pl.BlockSpec(memory_space=pltpu.VMEM)
    hbm = pl.BlockSpec(memory_space=pltpu.HBM)
    dma = pltpu.SemaphoreType.DMA
    return pl.pallas_call(
        kernel,
        out_shape=pltpu.VMEM((UNIT, examples), F32),
        in_specs=[hbm] * 5 + [pl.BlockSpec(memory_space=pltpu.SMEM)],
        out_specs=vmem,
        scratch_shapes=[
            pltpu.VMEM((count, width), BF16),
            pltpu.VMEM((examples, width), BF16),
            pltpu.VMEM((SIDE, SIDE), F32),
            pltpu.VMEM((SIDE, SIDE), F32),
            pltpu.SMEM(query_ids.shape, jnp.int32),
            pltpu.VMEM((2, 2, 512, 128), F32),
            pltpu.VMEM((2, 512, 128), F32),
            pltpu.VMEM((512, width), BF16),
            pltpu.VMEM((512, examples), BF16),
            pltpu.VMEM((8, 8, UNIT, examples), BF16),
            pltpu.VMEM((8, UNIT, examples), F32),
            pltpu.VMEM((4, UNIT, examples), F32),
            pltpu.VMEM((8, 128), F32),
            pltpu.VMEM((7, 8, 128), F32),
            pltpu.VMEM((4, 8, 128), F32),
            pltpu.VMEM((8, 128), F32),
            pltpu.VMEM((8, 128), F32),
            dma((8,)),
            dma((1,)),
            dma((32,)),
            dma((8,)),
            dma((8,)),
            dma((8,)),
            dma((4,)),
            dma((7,)),
            dma((7,)),
            dma((3,)),
            dma((3,)),
            dma((15,)),
            dma((1,)),
        ],
        compiler_params=pltpu.CompilerParams(
            collective_id=0, has_side_effects=True, vmem_limit_bytes=60 * 2**20
        ),
        cost_estimate=pl.CostEstimate(
            flops=2 * 512 * examples * width, bytes_accessed=(examples + count) * width * 2, transcendentals=0
        ),
    )(
        query_grads.reshape(count, width),
        store.reshape(examples, width),
        left_inv.reshape(SIDE, SIDE),
        right_inv.reshape(SIDE, SIDE),
        query_ids,
        block_offsets,
    )


def solution(mesh):
    return jax.shard_map(
        per_device,
        mesh=mesh,
        in_specs=(
            P("ex", "lay", None),
            P("ex", "lay", None),
            P("lay", None, None),
            P("lay", None, None),
            P(),
            P("ex"),
        ),
        out_specs=P("lay", "ex"),
        check_vma=False,
    )
```
